32 devices in a mesh: gx: 2 (over x), gy: 4 (over z), sa: 4 (over y, core).
Axes of the slice: x: 2, y: 2, z: 4, core: 2. Of those that a mesh axis runs over, the one named last changes fastest.
Arguments:
- scalar_field: float32 [64, 1, 1024, 512], P('sa', None, 'gx', 'gy'), may hold values from -80 to 80, as said below
- start_basis: float32 [1024, 128], replicated, may hold values from -6 to 6
Outputs:
- core_tensor: float32 [64, 1, 128, 512], P(('sa', 'gx'), None, 'gy')
- leading_basis: float32 [1024, 128], P(('gx', 'gy', 'sa'))
The draws below stay inside these ranges and needn't reach their ends.
Inputs may be any that keep to these rules, and one draw needn't show every extreme that they name: `scalar_field`: every entry is finite.
All inputs are finite; a program needn't handle non-finite values.
Results may differ from the reference program's by a relative error of at most 0.0003.
Values sent between devices are 32-bit elements; how exact they have to be, the bound alone decides.
No kernel may reach another device: no remote copies, remote signals or barrier semaphores. Data moves between devices by JAX's collectives and lax.ppermute only.
A program may use at most 64 MiB of HBM per device.

```python
import math
import jax
import jax.numpy as jnp
from jax import lax

NX = 1024
S = 64
R = 128
ITERS = 3
STEPS = 1
NY = 512


def draw_scalar_field(key, part):
    keys = jax.random.split(key, 5)
    shape = (S, STEPS, NX, NY)
    mode_count = R + R // 8
    decay = math.log(625.0) / (R - 1)
    floor_scale = math.sqrt(NX / 600.0)
    species_scale = jnp.exp(jax.random.uniform(keys[2], (S,), jnp.float32, 0.0, math.log(4.0)))
    noise = jnp.clip(jax.random.normal(keys[0], shape, jnp.float32), -4.0, 4.0)

    def add_mode(index, total):
        along_x = jnp.clip(jax.random.normal(jax.random.fold_in(keys[3], index), (NX,), jnp.float32), -3.0, 3.0)
        along_y = jnp.clip(jax.random.normal(jax.random.fold_in(keys[4], index), (S, STEPS, NY), jnp.float32), -3.0, 3.0)
        amplitude = jnp.exp(-0.5 * decay * index.astype(jnp.float32))
        return total + amplitude * along_y[:, :, None, :] * along_x[None, None, :, None]
    total = lax.fori_loop(0, mode_count, add_mode, floor_scale * noise)
    return jnp.clip(0.25 * total * species_scale[:, None, None, None], -80.0, 80.0)


def centred(stream_key, shape, scale, reach, dtype=jnp.bfloat16):
    result = jax.random.normal(stream_key, shape, jnp.float32) * scale
    return jnp.minimum(jnp.maximum(result, -reach), reach).astype(dtype)


def setup_inputs(seed: int = 0) -> dict:
    key_of = jax.random.split(jax.random.key(seed), 3)
    return {
        "scalar_field": draw_scalar_field(jax.random.fold_in(key_of[2], 71), 0),
        "start_basis": centred(key_of[1], (NX, R), 1.0, 6.0, jnp.float32),
    }


HIGHEST_PREC = lax.Precision.HIGHEST

def orthonormal(mapped):
    inner_gram = jnp.dot(mapped.T.astype(jnp.float32), mapped.astype(jnp.float32), precision=HIGHEST_PREC, preferred_element_type=jnp.float32)
    factor = jnp.linalg.cholesky(inner_gram)
    return jax.scipy.linalg.solve_triangular(factor, mapped.T, lower=True).T

def reference(scalar_field, start_basis):
    slabs = scalar_field.reshape(S * STEPS, NX, NY)

    def accumulate(carry, slab_now):
        return (carry + jnp.dot(slab_now.astype(jnp.float32), slab_now.T.astype(jnp.float32), precision=HIGHEST_PREC, preferred_element_type=jnp.float32), None)
    gram_matrix, _ = lax.scan(accumulate, jnp.zeros((NX, NX), jnp.float32), slabs)
    gram_matrix = gram_matrix / (NY * S * STEPS)
    cur_basis = start_basis
    for iteration in range(ITERS):
        mapped = jnp.dot(gram_matrix.astype(jnp.float32), cur_basis.astype(jnp.float32), precision=HIGHEST_PREC, preferred_element_type=jnp.float32)
        cur_basis = orthonormal(orthonormal(mapped))
    core_tensor = jnp.einsum('xk,stxy->stky', cur_basis.astype(jnp.float32), scalar_field.astype(jnp.float32), precision=HIGHEST_PREC, preferred_element_type=jnp.float32)
    return (core_tensor, cur_basis)
```

```python
import functools

import jax
import jax.numpy as jnp
from jax import lax
from jax.experimental import pallas as pl
from jax.experimental.pallas import tpu as pltpu
from jax.sharding import PartitionSpec as P

ITERS = 3
PANEL = 8
SMALL = 1e-6
HIGHEST_PREC = lax.Precision.HIGHEST
HIGH_PREC = lax.Precision.HIGH


def mul(left, right):
    return lax.dot_general(
        left, right, (((1,), (0,)), ((), ())), precision=HIGHEST_PREC, preferred_element_type=jnp.float32
    )


def mul_t(left, right):
    return lax.dot_general(
        left, right, (((1,), (1,)), ((), ())), precision=HIGHEST_PREC, preferred_element_type=jnp.float32
    )


def inverse_factor(matrix):
    order = matrix.shape[0]
    panels = order // PANEL
    shape = (PANEL, order)
    sub = lax.broadcasted_iota(jnp.int32, shape, 0)
    lane = lax.broadcasted_iota(jnp.int32, shape, 1)
    rows = [matrix[PANEL * q : PANEL * (q + 1), :] for q in range(panels)]
    inverse = [jnp.where(lane == sub + PANEL * q, 1.0, 0.0).astype(jnp.float32) for q in range(panels)]
    for p in range(panels):
        columns = {
            q: [
                jnp.broadcast_to(rows[q][:, PANEL * p + j : PANEL * p + j + 1], shape)
                for j in range(PANEL)
            ]
            for q in range(p, panels)
        }
        for j in range(PANEL):
            scale = lax.rsqrt(jnp.broadcast_to(columns[p][j][j : j + 1, :], shape))
            factor = {q: columns[q][j] * scale for q in range(p, panels)}
            row = jnp.broadcast_to(rows[p][j : j + 1, :], shape) * scale
            inverse_row = jnp.broadcast_to(inverse[p][j : j + 1, :], shape) * scale
            for k in range(j + 1, PANEL):
                pivot = jnp.broadcast_to(factor[p][k : k + 1, :], shape)
                for q in range(p, panels):
                    columns[q][k] = columns[q][k] - factor[q] * pivot
            below = jnp.where(sub > j, factor[p], 0.0)
            rows[p] = rows[p] - below * row
            inverse[p] = jnp.where(sub == j, inverse_row, inverse[p] - below * inverse_row)
            for q in range(p + 1, panels):
                rows[q] = rows[q] - factor[q] * row
                inverse[q] = inverse[q] - factor[q] * inverse_row
    return jnp.concatenate(inverse, axis=0)


def inverse_factor_near_one(error, row, col):
    def lower(a):
        return jnp.where(row > col, a, jnp.where(row == col, 0.5 * a, 0.0))

    first = lower(error)
    eye = jnp.where(row == col, 1.0, 0.0)
    return eye - first + (lower(mul_t(first, first)) + mul(first, first))


def subspace_kernel(first_ref, last_ref, cross_ref, start_ref, basis_ref, gram_ref, inverse_ref):
    half = first_ref.shape[0]
    rank = start_ref.shape[0]
    row = lax.broadcasted_iota(jnp.int32, (rank, rank), 0)
    col = lax.broadcasted_iota(jnp.int32, (rank, rank), 1)
    cross = cross_ref[...]
    gram_ref[:half, :half] = first_ref[...]
    gram_ref[half:, half:] = last_ref[...]
    gram_ref[:half, half:] = cross
    gram_ref[half:, :half] = cross.T
    basis_ref[...] = start_ref[...]

    def iteration(_, carry):
        mapped = mul(basis_ref[...], gram_ref[...])
        once = mul(inverse_factor(mul_t(mapped, mapped)), mapped)
        inner = mul_t(once, once)
        error = inner - jnp.where(row == col, 1.0, 0.0)
        small = jnp.sum(error * error) <= SMALL

        @pl.when(small)
        def _():
            inverse_ref[...] = inverse_factor_near_one(error, row, col)

        @pl.when(jnp.logical_not(small))
        def _():
            inverse_ref[...] = inverse_factor(inner)

        basis_ref[...] = mul(inverse_ref[...], once)
        return carry

    lax.fori_loop(0, ITERS, iteration, 0)


def subspace(first, last, cross, start):
    rank, order = start.shape
    return pl.pallas_call(
        subspace_kernel,
        out_shape=jax.ShapeDtypeStruct((rank, order), jnp.float32),
        in_specs=[pl.BlockSpec(memory_space=pltpu.VMEM)] * 4,
        out_specs=pl.BlockSpec(memory_space=pltpu.VMEM),
        scratch_shapes=[pltpu.VMEM((order, order), jnp.float32), pltpu.VMEM((rank, rank), jnp.float32)],
        compiler_params=pltpu.CompilerParams(vmem_limit_bytes=48 << 20),
        name="subspace",
    )(first, last, cross, start)


def flip(size, bit):
    return [(i, i ^ bit) for i in range(size)]


def turn(size, step):
    return [(i, (i + step) % size) for i in range(size)]


def blocks(array, count):
    return array.reshape((count, array.shape[0] // count) + array.shape[1:])


def part(array, index):
    return lax.dynamic_index_in_dim(array, index, 0, keepdims=False)


def scatter_flip(array, axis, bit):
    mine = (lax.axis_index(axis) & bit) // bit
    halves = blocks(array, 2)
    got = lax.ppermute(part(halves, 1 - mine), axis, flip(lax.axis_size(axis), bit))
    return part(halves, mine) + got


def gather_flip(array, axis, bit):
    mine = (lax.axis_index(axis) & bit) // bit
    got = lax.ppermute(array, axis, flip(lax.axis_size(axis), bit))
    low = jnp.where(mine == 0, array, got)
    high = jnp.where(mine == 0, got, array)
    return jnp.concatenate([low, high], axis=0)


def scatter_turn(array, axis):
    size = lax.axis_size(axis)
    mine = lax.axis_index(axis)
    parts = blocks(array, size)
    total = part(parts, mine)
    for step in range(1, size):
        total = total + lax.ppermute(part(parts, (mine + step) % size), axis, turn(size, step))
    return total


def gather_turn(array, axis):
    size = lax.axis_size(axis)
    mine = lax.axis_index(axis)
    out = jnp.zeros((size,) + array.shape, array.dtype)
    out = lax.dynamic_update_index_in_dim(out, array, mine, 0)
    for step in range(1, size):
        got = lax.ppermute(array, axis, turn(size, step))
        out = lax.dynamic_update_index_in_dim(out, got, (mine - step) % size, 0)
    return out.reshape((-1,) + array.shape[1:])


def pair_targets(size):
    moves = [(1, 0), (0, 2), (1, 2)]
    return [
        [(x * size + s, (x ^ dx) * size + (s ^ ds)) for x in range(2) for s in range(size)]
        for dx, ds in moves
    ], moves


def sum_cross(array):
    rows = array.shape[0]
    quarter = scatter_flip(array, "sa", 1)
    targets, moves = pair_targets(lax.axis_size("sa"))
    x = lax.axis_index("gx")
    y = lax.axis_index("sa") // 2
    parts = blocks(quarter, 4)
    total = part(parts, x * 2 + y)
    for target, (dx, ds) in zip(targets, moves):
        total = total + lax.ppermute(
            part(parts, (x ^ dx) * 2 + (y ^ (ds // 2))), ("gx", "sa"), target
        )
    size = lax.axis_size("gy")
    shares = [lax.ppermute(total, "gy", turn(size, step)) for step in range(1, size)]
    for share in shares:
        total = total + share
    out = jnp.zeros((4,) + total.shape, total.dtype)
    out = lax.dynamic_update_index_in_dim(out, total, x * 2 + y, 0)
    for target, (dx, ds) in zip(targets, moves):
        got = lax.ppermute(total, ("gx", "sa"), target)
        out = lax.dynamic_update_index_in_dim(out, got, (x ^ dx) * 2 + (y ^ (ds // 2)), 0)
    return gather_flip(out.reshape((rows // 2,) + array.shape[1:]), "sa", 1)


def sum_own(array):
    rows, cols = array.shape
    piece = scatter_turn(scatter_flip(scatter_flip(array, "sa", 1), "sa", 2), "gy")
    other = lax.ppermute(piece, "gx", flip(2, 1))
    both = jnp.concatenate([piece, other], axis=1)
    whole = gather_flip(gather_flip(gather_turn(both, "gy"), "sa", 2), "sa", 1)
    x = lax.axis_index("gx")
    own, far = whole[:, :cols], whole[:, cols:]
    return jnp.where(x == 0, own, far), jnp.where(x == 0, far, own)


def outer(left, right):
    return jnp.einsum(
        "stxy,stzy->xz", left, right, precision=HIGH_PREC, preferred_element_type=jnp.float32
    )


def project(basis, field):
    return jnp.einsum(
        "kx,stxy->stky", basis, field, precision=HIGH_PREC, preferred_element_type=jnp.float32
    )


def on_halves(field, start):
    x = lax.axis_index("gx")
    species = field.shape[0] // 2
    half = field.shape[2]
    columns = field.shape[0] * field.shape[1] * field.shape[3]
    columns = columns * lax.axis_size("gy") * lax.axis_size("sa")
    mine = lax.dynamic_slice_in_dim(field, x * species, species, 0)
    sent = lax.dynamic_slice_in_dim(field, (1 - x) * species, species, 0)
    count = 4
    received = [lax.ppermute(piece, "gx", flip(2, 1)) for piece in blocks(sent, count)]
    first, last = sum_own(outer(field, field))
    cross = 0.0
    for got, kept in zip(received, blocks(mine, count)):
        cross = cross + outer(jnp.where(x == 0, kept, got), jnp.where(x == 0, got, kept))
    cross = sum_cross(cross)
    basis = subspace(first / columns, last / columns, cross / columns, start.T)
    near = lax.dynamic_slice_in_dim(basis, x * half, half, 1)
    far = lax.dynamic_slice_in_dim(basis, (1 - x) * half, half, 1)
    projected = project(near, mine) + project(far, jnp.concatenate(received, axis=0))
    return basis, projected


def on_fibres(field, start):
    fibres = lax.all_to_all(field, "gx", split_axis=0, concat_axis=2, tiled=True)
    columns = fibres.shape[0] * fibres.shape[1] * fibres.shape[3]
    columns = columns * lax.axis_size(("gx", "gy", "sa"))
    half = fibres.shape[2] // 2
    gram = lax.psum(outer(fibres, fibres), ("gx", "gy", "sa")) / columns
    basis = subspace(gram[:half, :half], gram[half:, half:], gram[:half, half:], start.T)
    return basis, project(basis, fibres)


def on_device(scalar_field, start_basis):
    if lax.axis_size("gx") == 2 and lax.axis_size("sa") == 4:
        basis, projected = on_halves(scalar_field, start_basis)
    else:
        basis, projected = on_fibres(scalar_field, start_basis)
    rows_dev = start_basis.shape[0] // lax.axis_size(("gx", "gy", "sa"))
    my_index = lax.axis_index(("gx", "gy", "sa"))
    own_rows = lax.dynamic_slice_in_dim(basis.T, my_index * rows_dev, rows_dev, 0)
    core_tensor = lax.all_to_all(projected, "gy", split_axis=2, concat_axis=3, tiled=True)
    return (core_tensor, own_rows)


def solution(mesh):
    placed = (P("sa", None, "gx", "gy"), P())
    return jax.shard_map(
        on_device,
        mesh=mesh,
        in_specs=placed,
        out_specs=(P(("sa", "gx"), None, "gy", None), P(("gx", "gy", "sa"), None)),
        check_vma=False,
    )
```

```python
import functools
import math

import jax
import jax.numpy as jnp
from jax import lax
from jax.experimental import pallas as pl
from jax.experimental.pallas import tpu as pltpu
from jax.sharding import PartitionSpec as P

ITERS = 3
PANEL = 8
SMALL = 1e-6
HIGHEST_PREC = lax.Precision.HIGHEST
HIGH_PREC = lax.Precision.HIGH


def mul(left, right):
    return lax.dot_general(
        left, right, (((1,), (0,)), ((), ())), precision=HIGHEST_PREC, preferred_element_type=jnp.float32
    )


def mul_t(left, right):
    return lax.dot_general(
        left, right, (((1,), (1,)), ((), ())), precision=HIGHEST_PREC, preferred_element_type=jnp.float32
    )


def inverse_factor(matrix):
    order = matrix.shape[0]
    panels = order // PANEL
    shape = (PANEL, order)
    sub = lax.broadcasted_iota(jnp.int32, shape, 0)
    lane = lax.broadcasted_iota(jnp.int32, shape, 1)
    rows = [matrix[PANEL * q : PANEL * (q + 1), :] for q in range(panels)]
    inverse = [jnp.where(lane == sub + PANEL * q, 1.0, 0.0).astype(jnp.float32) for q in range(panels)]
    for p in range(panels):
        columns = {
            q: [
                jnp.broadcast_to(rows[q][:, PANEL * p + j : PANEL * p + j + 1], shape)
                for j in range(PANEL)
            ]
            for q in range(p, panels)
        }
        for j in range(PANEL):
            scale = lax.rsqrt(jnp.broadcast_to(columns[p][j][j : j + 1, :], shape))
            factor = {q: columns[q][j] * scale for q in range(p, panels)}
            row = jnp.broadcast_to(rows[p][j : j + 1, :], shape) * scale
            inverse_row = jnp.broadcast_to(inverse[p][j : j + 1, :], shape) * scale
            for k in range(j + 1, PANEL):
                pivot = jnp.broadcast_to(factor[p][k : k + 1, :], shape)
                for q in range(p, panels):
                    columns[q][k] = columns[q][k] - factor[q] * pivot
            below = jnp.where(sub > j, factor[p], 0.0)
            rows[p] = rows[p] - below * row
            inverse[p] = jnp.where(sub == j, inverse_row, inverse[p] - below * inverse_row)
            for q in range(p + 1, panels):
                rows[q] = rows[q] - factor[q] * row
                inverse[q] = inverse[q] - factor[q] * inverse_row
    return jnp.concatenate(inverse, axis=0)


def inverse_factor_near_one(error, row, col):
    def lower(a):
        return jnp.where(row > col, a, jnp.where(row == col, 0.5 * a, 0.0))

    first = lower(error)
    eye = jnp.where(row == col, 1.0, 0.0)
    return eye - first + (lower(mul_t(first, first)) + mul(first, first))


def iterate(start_ref, basis_ref, gram_ref, inverse_ref):
    rank = start_ref.shape[0]
    row = lax.broadcasted_iota(jnp.int32, (rank, rank), 0)
    col = lax.broadcasted_iota(jnp.int32, (rank, rank), 1)
    basis_ref[...] = start_ref[...]

    def iteration(_, carry):
        mapped = mul(basis_ref[...], gram_ref[...])
        once = mul(inverse_factor(mul_t(mapped, mapped)), mapped)
        inner = mul_t(once, once)
        error = inner - jnp.where(row == col, 1.0, 0.0)
        small = jnp.sum(error * error) <= SMALL

        @pl.when(small)
        def _():
            inverse_ref[...] = inverse_factor_near_one(error, row, col)

        @pl.when(jnp.logical_not(small))
        def _():
            inverse_ref[...] = inverse_factor(inner)

        basis_ref[...] = mul(inverse_ref[...], once)
        return carry

    lax.fori_loop(0, ITERS, iteration, 0)


VMEM_SPEC = pl.BlockSpec(memory_space=pltpu.VMEM)
SMEM_SPEC = pl.BlockSpec(memory_space=pltpu.SMEM)


def params(mebibytes):
    return pltpu.CompilerParams(vmem_limit_bytes=mebibytes << 20)


def whole_kernel(gram_ref, start_ref, basis_ref, inverse_ref):
    iterate(start_ref, basis_ref, gram_ref, inverse_ref)


def subspace_whole(gram, start):
    rank, order = start.shape
    return pl.pallas_call(
        whole_kernel,
        out_shape=jax.ShapeDtypeStruct((rank, order), jnp.float32),
        in_specs=[VMEM_SPEC] * 2,
        out_specs=VMEM_SPEC,
        scratch_shapes=[pltpu.VMEM((rank, rank), jnp.float32)],
        compiler_params=params(24),
        name="subspace_whole",
    )(gram, start)


def pieces_kernel(scale, place_ref, *refs):
    own_refs, cross_refs = refs[:8], refs[8:16]
    start_ref, basis_ref, gram_ref, packed_ref, inverse_ref = refs[16:]
    x, y, core = place_ref[0], place_ref[1], place_ref[2]
    half = gram_ref.shape[0] // 2
    side = half // 2
    rows = own_refs[0].shape[0]
    for ref, (dc, dx, dy) in zip(own_refs, PIECES):
        at = pl.multiple_of(((core ^ dc) * 2 + (y ^ dy)) * rows, 8)
        packed_ref[x ^ dx, pl.ds(at, rows), :] = ref[...]
    rows = cross_refs[0].shape[0]
    for ref, (dc, dx, dy) in zip(cross_refs, PIECES):
        at = pl.multiple_of(((core ^ dc) * 4 + (x ^ dx) * 2 + (y ^ dy)) * rows, 8)
        gram_ref[pl.ds(at, rows), half:] = ref[...] * scale
    gram_ref[half:, :half] = gram_ref[:half, half:].T
    for p in range(2):
        base = p * half
        top = side // 2
        low = packed_ref[p, top:, :] * scale
        gram_ref[base : base + top, base : base + side] = packed_ref[p, :top, :side] * scale
        gram_ref[base + top : base + side, base : base + side] = packed_ref[p, :top, side:] * scale
        gram_ref[base + side : base + half, base : base + half] = low
        gram_ref[base : base + side, base + side : base + half] = low[:, :side].T
    iterate(start_ref, basis_ref, gram_ref, inverse_ref)


PIECES = [(dc, dx, dy) for dc in range(2) for dx, dy in ((0, 0), (1, 0), (0, 1), (1, 1))]


def subspace_pieces(place, own, cross, start, scale):
    rank, order = start.shape
    half = order // 2
    return pl.pallas_call(
        functools.partial(pieces_kernel, scale),
        out_shape=jax.ShapeDtypeStruct((rank, order), jnp.float32),
        in_specs=[SMEM_SPEC] + [VMEM_SPEC] * 17,
        out_specs=VMEM_SPEC,
        scratch_shapes=[
            pltpu.VMEM((order, order), jnp.float32),
            pltpu.VMEM((2, 3 * half // 4, half), jnp.float32),
            pltpu.VMEM((rank, rank), jnp.float32),
        ],
        compiler_params=params(56),
        name="subspace",
    )(place, *own, *cross, start)


def split(value):
    high = value.astype(jnp.bfloat16)
    return high, (value - high.astype(jnp.float32)).astype(jnp.bfloat16)


def dot3(left, right, contract):
    (a, b), (c, d) = left, right

    def dot(u, v):
        return lax.dot_general(u, v, (contract, ((), ())), preferred_element_type=jnp.float32)

    return dot(a, c) + (dot(a, d) + dot(b, c))


CORNERS = ((1, 0), (0, 1), (1, 1))
NN = ((1,), (0,))
NT = ((1,), (1,))


def pick(parts, rows):
    return parts[0][rows], parts[1][rows]


def own_kernel(place_ref, field_ref, keep_ref, send_ref, total_ref):
    half = field_ref.shape[2]
    side = half // 2
    top = side // 2
    values = split(jnp.concatenate([field_ref[s, 0] for s in range(field_ref.shape[0])], axis=1))
    upper = pick(values, slice(0, side))
    lower = pick(values, slice(side, half))

    @pl.when(pl.program_id(0) == 0)
    def _():
        total_ref[...] = jnp.zeros_like(total_ref)

    square = dot3(upper, upper, NT)
    total_ref[:top, :side] += square[:top]
    total_ref[:top, side:] += square[top:]
    total_ref[top:, :] += dot3(lower, values, NT)

    @pl.when(pl.program_id(0) == pl.num_programs(0) - 1)
    def _():
        rows = keep_ref.shape[0]
        core = place_ref[2]
        keep_ref[...] = total_ref[pl.ds(pl.multiple_of(core * rows, 8), rows), :]
        send_ref[...] = total_ref[pl.ds(pl.multiple_of((1 - core) * rows, 8), rows), :]


def own_blocks(place, field):
    half = field.shape[2]
    rows = 3 * half // 4
    step = math.gcd(field.shape[0], 4)
    shape = jax.ShapeDtypeStruct((rows // 2, half), jnp.float32)
    return pl.pallas_call(
        own_kernel,
        grid=(field.shape[0] // step,),
        out_shape=[shape, shape],
        in_specs=[SMEM_SPEC, pl.BlockSpec((step, 1, half, field.shape[3]), lambda i: (i, 0, 0, 0))],
        out_specs=[pl.BlockSpec((rows // 2, half), lambda i: (0, 0))] * 2,
        scratch_shapes=[pltpu.VMEM((rows, half), jnp.float32)],
        compiler_params=params(56),
        cost_estimate=pl.CostEstimate(flops=2 * 10**11, bytes_accessed=field.size * 4, transcendentals=0),
        name="own_blocks",
    )(place, field)


def species_pairs(refs):
    slots = [(i, s) for i, ref in enumerate(refs) for s in range(ref.shape[0])]
    return [slots[i : i + 2] for i in range(0, len(slots), 2)]


def cross_kernel(count, last, place_ref, *refs):
    got_refs, kept_refs = refs[:count], refs[count : 2 * count]
    refs = refs[2 * count :]
    x, core = place_ref[0], place_ref[2]
    half = got_refs[0].shape[2]
    rows = half // 2
    in_order = x == 0

    def product(at):
        total = None
        some, every = pl.ds(at, rows), slice(None)
        for pair in species_pairs(got_refs):
            def two(refs, where):
                return jnp.concatenate([refs[i][s, 0, where, :] for i, s in pair], axis=1)

            low = split(jnp.where(in_order, two(kept_refs, some), two(got_refs, some)))
            high = split(jnp.where(in_order, two(got_refs, every), two(kept_refs, every)))
            value = dot3(low, high, NT)
            total = value if total is None else total + value
        return total

    keep_at = pl.multiple_of(core * rows, 8)
    send_at = pl.multiple_of((1 - core) * rows, 8)
    if last:
        so_far_keep, so_far_send, keep_ref, send_ref = refs
        send_ref[...] = so_far_send[...] + product(send_at)
        keep_ref[...] = so_far_keep[...] + product(keep_at)
    else:
        keep_ref, send_ref = refs
        send_ref[...] = product(send_at)
        keep_ref[...] = product(keep_at)


def cross_block(place, got, kept, so_far):
    half = got[0].shape[2]
    shape = jax.ShapeDtypeStruct((half // 2, half), jnp.float32)
    return pl.pallas_call(
        functools.partial(cross_kernel, len(got), bool(so_far)),
        out_shape=[shape, shape],
        in_specs=[SMEM_SPEC] + [VMEM_SPEC] * (2 * len(got) + len(so_far)),
        out_specs=[VMEM_SPEC] * 2,
        compiler_params=params(24),
        name="cross_block",
    )(place, *got, *kept, *so_far)


def quarters_kernel(place_ref, left_ref, right_ref, *out_refs):
    rows = out_refs[0].shape[0]
    x, y = place_ref[0], place_ref[1]
    for ref, (dx, dy) in zip(out_refs, ((0, 0),) + CORNERS):
        some = pl.ds(pl.multiple_of(((x ^ dx) * 2 + (y ^ dy)) * rows, 8), rows)
        ref[...] = left_ref[some, :] + right_ref[some, :]


def sum_quarters(place, left, right):
    shape = jax.ShapeDtypeStruct((left.shape[0] // 4, left.shape[1]), jnp.float32)
    return pl.pallas_call(
        quarters_kernel,
        out_shape=[shape] * 4,
        in_specs=[SMEM_SPEC] + [VMEM_SPEC] * 2,
        out_specs=[VMEM_SPEC] * 4,
        compiler_params=params(24),
        name="quarters",
    )(place, left, right)


def project_kernel(count, place_ref, basis_ref, *refs):
    got_refs, kept_refs = refs[:count], refs[count : 2 * count]
    own_rows_ref, slab_refs, value_ref = refs[2 * count], refs[2 * count + 1 : -1], refs[-1]
    x, z, index = place_ref[0], place_ref[3], place_ref[4]
    half = got_refs[0].shape[2]
    width = got_refs[0].shape[3]
    near = split(basis_ref[:, pl.ds(pl.multiple_of(x * half, 128), half)])
    far = split(basis_ref[:, pl.ds(pl.multiple_of((1 - x) * half, 128), half)])
    slabs = len(slab_refs)
    rows = slab_refs[0].shape[2]
    for number, pair in enumerate(species_pairs(got_refs)):
        def two(refs):
            return split(jnp.concatenate([refs[i][s, 0] for i, s in pair], axis=1))

        value_ref[...] = dot3(near, two(kept_refs), NN) + dot3(far, two(got_refs), NN)
        for step in range(slabs):
            at = pl.multiple_of(lax.rem(z + step, slabs) * rows, 8)
            for j in range(len(pair)):
                slab_refs[step][2 * number + j, 0] = value_ref[
                    pl.ds(at, rows), width * j : width * (j + 1)
                ]
    count_rows = own_rows_ref.shape[0]
    per_tile = 128 // count_rows
    tile = basis_ref[:, pl.ds(pl.multiple_of(index // per_tile * 128, 128), 128)].T
    shift = lax.rem(index, per_tile)
    value_ref[:, :width] = tile
    own_rows_ref[...] = value_ref[pl.ds(pl.multiple_of(shift * count_rows, 8), count_rows), :width]


def project_slabs(place, basis, got, kept, slabs, own_rows):
    rank = basis.shape[0]
    species = sum(piece.shape[0] for piece in got)
    width = got[0].shape[3]
    slab = jax.ShapeDtypeStruct((species, 1, rank // slabs, width), jnp.float32)
    rows = jax.ShapeDtypeStruct((own_rows, rank), jnp.float32)
    return pl.pallas_call(
        functools.partial(project_kernel, len(got)),
        out_shape=[rows] + [slab] * slabs,
        in_specs=[SMEM_SPEC] + [VMEM_SPEC] * (1 + 2 * len(got)),
        out_specs=[VMEM_SPEC] * (1 + slabs),
        scratch_shapes=[pltpu.VMEM((rank, 2 * width), jnp.float32)],
        compiler_params=params(24),
        name="project",
    )(place, basis, *got, *kept)


def join_kernel(place_ref, *refs):
    out_ref = refs[-1]
    slabs = len(refs) - 1
    width = refs[0].shape[3]
    for step in range(slabs):
        source = lax.rem(place_ref[3] + slabs - step, slabs)
        out_ref[:, :, :, pl.ds(pl.multiple_of(source * width, 128), width)] = refs[step][...]


def join_slabs(place, slabs):
    shape = slabs[0].shape[:3] + (slabs[0].shape[3] * len(slabs),)
    return pl.pallas_call(
        join_kernel,
        out_shape=jax.ShapeDtypeStruct(shape, jnp.float32),
        in_specs=[SMEM_SPEC] + [VMEM_SPEC] * len(slabs),
        out_specs=VMEM_SPEC,
        compiler_params=params(24),
        name="join",
    )(place, *slabs)


def blocks(array, count):
    return array.reshape((count, array.shape[0] // count) + array.shape[1:])


def part(array, index):
    return lax.dynamic_index_in_dim(array, index, 0, keepdims=False)


def flip(size, bit):
    return [(i, i ^ bit) for i in range(size)]


def turn(size, step):
    return [(i, (i + step) % size) for i in range(size)]


def after(value, *others):
    return lax.optimization_barrier((value, others))[0]


def send_core(array):
    return lax.ppermute(array, "sa", flip(lax.axis_size("sa"), 1))


def send_corner(array, dx, dy):
    size = lax.axis_size("sa")
    pairs = [(x * size + s, (x ^ dx) * size + (s ^ (2 * dy))) for x in range(2) for s in range(size)]
    return lax.ppermute(array, ("gx", "sa"), pairs)


def sum_z(array):
    size = lax.axis_size("gy")
    shares = [lax.ppermute(array, "gy", turn(size, step)) for step in range(1, size)]
    return sum(shares, array)


def gather_pieces(array):
    near = [array] + [send_corner(array, dx, dy) for dx, dy in CORNERS]
    return near + [send_core(piece) for piece in near]


def chunk_sizes(species):
    return [3, species - 5, 2]


def on_halves(field, start):
    x = lax.axis_index("gx")
    y = lax.axis_index("sa") // 2
    core = lax.axis_index("sa") % 2
    z = lax.axis_index("gy")
    place = jnp.stack([x, y, core, z, lax.axis_index(("gx", "gy", "sa"))]).astype(jnp.int32)
    species = field.shape[0] // 2
    columns = field.shape[0] * field.shape[1] * field.shape[3]
    columns = columns * lax.axis_size("gy") * lax.axis_size("sa")
    sizes = chunk_sizes(species)
    starts = [sum(sizes[:i]) for i in range(len(sizes))]

    def chunk(source, owner, i):
        return lax.dynamic_slice_in_dim(source, owner * species + starts[i], sizes[i], 0)

    sent = [chunk(field, 1 - x, 0)]
    rest = after(field, sent[0])
    sent = sent + [chunk(rest, 1 - x, i) for i in range(1, len(sizes))]
    got = [lax.ppermute(piece, "gx", flip(2, 1)) for piece in sent]

    own_field = after(rest, sent)
    own_keep, own_send = own_blocks(place, own_field)
    own = blocks(own_keep + send_core(after(own_send, got[0])), 2)
    own = sum_z(part(own, y) + send_corner(part(own, 1 - y), 0, 1))

    kept = [chunk(own_field, x, i) for i in range(len(sizes))]
    start_t = start.T
    *early_got, final_got = got
    kept[0] = after(kept[0], start_t)
    so_far = cross_block(place, early_got, kept[:-1], ())
    final_got = after(final_got, own, so_far)
    cross_keep, cross_send = cross_block(place, [final_got], kept[-1:], so_far)
    cross, *shares = sum_quarters(place, cross_keep, send_core(cross_send))
    shares = [send_corner(share, dx, dy) for share, (dx, dy) in zip(shares, CORNERS)]
    cross = sum(shares, cross)
    own_pieces = gather_pieces(after(own, cross))
    cross_pieces = gather_pieces(sum_z(cross))

    basis = subspace_pieces(place, own_pieces, cross_pieces, start_t, 1.0 / columns)
    devices = lax.axis_size(("gx", "gy", "sa"))
    slabs = lax.axis_size("gy")
    own_rows, *projected = project_slabs(
        place, basis, early_got + [final_got], kept, slabs, start.shape[0] // devices
    )
    arrived = [projected[0]] + [
        lax.ppermute(projected[i], "gy", turn(slabs, i)) for i in range(1, slabs)
    ]
    return join_slabs(place, arrived), own_rows


def outer(left, right):
    return jnp.einsum(
        "stxy,stzy->xz", left, right, precision=HIGH_PREC, preferred_element_type=jnp.float32
    )


def on_fibres(field, start):
    axes = ("gx", "gy", "sa")
    fibres = lax.all_to_all(field, "gx", split_axis=0, concat_axis=2, tiled=True)
    columns = fibres.shape[0] * fibres.shape[1] * fibres.shape[3] * lax.axis_size(axes)
    gram = lax.psum(outer(fibres, fibres), axes) / columns
    basis = subspace_whole(gram, start.T)
    projected = jnp.einsum(
        "kx,stxy->stky", basis, fibres, precision=HIGH_PREC, preferred_element_type=jnp.float32
    )
    rows_dev = start.shape[0] // lax.axis_size(axes)
    own_rows = lax.dynamic_slice_in_dim(basis.T, lax.axis_index(axes) * rows_dev, rows_dev, 0)
    return lax.all_to_all(projected, "gy", split_axis=2, concat_axis=3, tiled=True), own_rows


def on_device(scalar_field, start_basis):
    if lax.axis_size("gx") == 2 and lax.axis_size("sa") == 4:
        return on_halves(scalar_field, start_basis)
    return on_fibres(scalar_field, start_basis)


def solution(mesh):
    placed = (P("sa", None, "gx", "gy"), P())
    return jax.shard_map(
        on_device,
        mesh=mesh,
        in_specs=placed,
        out_specs=(P(("sa", "gx"), None, "gy", None), P(("gx", "gy", "sa"), None)),
        check_vma=False,
    )
```

```python
import functools
import math

import jax
import jax.numpy as jnp
from jax import lax
from jax.experimental import pallas as pl
from jax.experimental.pallas import tpu as pltpu
from jax.sharding import PartitionSpec as P

ITERS = 3
CORNERS = ((1, 0), (0, 1), (1, 1))
PANEL = 8
AHEAD = 3
SMALL = 1e-6
MEDIUM = 4e-4
NN = ((1,), (0,))
NT = ((1,), (1,))
HIGHEST_PREC = lax.Precision.HIGHEST
HIGH_PREC = lax.Precision.HIGH


def mul(left, right):
    return lax.dot_general(
        left, right, (((1,), (0,)), ((), ())), precision=HIGHEST_PREC, preferred_element_type=jnp.float32
    )


def mul_t(left, right):
    return lax.dot_general(
        left, right, (((1,), (1,)), ((), ())), precision=HIGHEST_PREC, preferred_element_type=jnp.float32
    )


def three_parts(value):
    high = value.astype(jnp.bfloat16)
    rest = value - high.astype(jnp.float32)
    middle = rest.astype(jnp.bfloat16)
    return high, middle, (rest - middle.astype(jnp.float32)).astype(jnp.bfloat16)


def inverse_factor(matrix):
    order = matrix.shape[0]
    panels = order // PANEL
    shape = (PANEL, order)
    sub = lax.broadcasted_iota(jnp.int32, shape, 0)
    lane = lax.broadcasted_iota(jnp.int32, shape, 1)
    rows = [matrix[PANEL * q : PANEL * (q + 1), :] for q in range(panels)]

    def spread(q, p):
        return [
            jnp.broadcast_to(rows[q][:, PANEL * p + j : PANEL * p + j + 1], shape) for j in range(PANEL)
        ]

    def sublane(value, k):
        return jnp.broadcast_to(value[k : k + 1, :], shape)

    following = spread(0, 0)
    for p in range(panels):
        near = list(range(p + 1, min(p + 1 + AHEAD, panels)))
        columns = {q: spread(q, p) for q in near}
        columns[p] = following
        following = spread(p + 1, p + 1) if near else []
        inside = (lane >= PANEL * p) & (lane < PANEL * (p + 1))
        rows[p] = jnp.where(inside, jnp.where(lane == sub + PANEL * p, 1.0, 0.0), rows[p])
        for q in range(p + 1, panels):
            rows[q] = jnp.where(inside, 0.0, rows[q])
        for j in range(PANEL):
            scale = lax.rsqrt(sublane(columns[p][j], j))
            factor = {q: columns[q][j] * scale for q in [p] + near}
            row = sublane(rows[p], j) * scale
            for k in range(j + 1, PANEL):
                pivot = sublane(factor[p], k)
                for q in [p] + near:
                    columns[q][k] = columns[q][k] - factor[q] * pivot
            for k in range(len(following)):
                following[k] = following[k] - factor[p + 1] * sublane(factor[p + 1], k)
            below = jnp.where(sub > j, factor[p], 0.0)
            rows[p] = jnp.where(sub == j, row, rows[p] - below * row)
            for q in near:
                rows[q] = rows[q] - factor[q] * row
        if p + 1 + AHEAD < panels:
            high, middle, low = (part.astype(jnp.float32) for part in three_parts(rows[p]))
            left = jnp.concatenate([high, high, high, middle, middle, low], axis=0)
            right = jnp.concatenate([high, middle, low, high, middle, high], axis=0)
            update = lax.dot_general(
                left.astype(jnp.bfloat16),
                right.astype(jnp.bfloat16),
                (((0,), (0,)), ((), ())),
                preferred_element_type=jnp.float32,
            )
            for q in range(p + 1 + AHEAD, panels):
                rows[q] = rows[q] - update[PANEL * q : PANEL * (q + 1), :]
    return jnp.concatenate(
        [jnp.where(lane <= sub + PANEL * q, rows[q], 0.0) for q in range(panels)], axis=0
    )


def lower(matrix, row, col):
    return jnp.where(row > col, matrix, jnp.where(row == col, 0.5 * matrix, 0.0))


def inverse_factor_near_one(error, row, col):
    first = lower(error, row, col)
    eye = jnp.where(row == col, 1.0, 0.0)
    return eye - first + (lower(mul_t(first, first), row, col) + mul(first, first))


def dot_t(left, right):
    return lax.dot_general(left, right, (NT, ((), ())), preferred_element_type=jnp.float32)


def inner_products(value):
    high, middle, low = three_parts(value)
    mixed = dot_t(high, middle) + dot_t(high, low)
    return dot_t(high, high) + ((mixed + mixed.T) + dot_t(middle, middle))


def apply(factor, value):
    a, b, c = three_parts(factor)
    high, middle, low = three_parts(value)

    def pass_of(left, right):
        return lax.dot_general(
            jnp.concatenate(left, axis=1),
            jnp.concatenate(right, axis=0),
            (NN, ((), ())),
            preferred_element_type=jnp.float32,
        )

    return pass_of([a, b], [high, middle]) + (
        pass_of([a, b], [middle, high]) + pass_of([a, c], [low, high])
    )


def iterate(scale, start_ref, basis_ref, gram_ref, inverse_ref):
    rank = start_ref.shape[0]
    row = lax.broadcasted_iota(jnp.int32, (rank, rank), 0)
    col = lax.broadcasted_iota(jnp.int32, (rank, rank), 1)
    eye = jnp.where(row == col, 1.0, 0.0)
    basis_ref[...] = start_ref[...]

    def iteration(_, carry):
        mapped = mul(basis_ref[...], gram_ref[...]) * scale
        once = apply(inverse_factor(inner_products(mapped)), mapped)
        inner = inner_products(once)
        error = inner - eye
        size = jnp.sum(error * error)

        @pl.when(size <= MEDIUM)
        def _():
            inverse_ref[...] = inverse_factor_near_one(error, row, col)

        @pl.when(jnp.logical_and(size > SMALL, size <= MEDIUM))
        def _():
            about = inverse_ref[...]
            rest = mul_t(mul(about, inner), about) - eye
            inverse_ref[...] = about - mul(lower(rest, row, col), about)

        @pl.when(jnp.logical_not(size <= MEDIUM))
        def _():
            inverse_ref[...] = inverse_factor(inner)

        basis_ref[...] = apply(inverse_ref[...], once)
        return carry

    lax.fori_loop(0, ITERS, iteration, 0)


VMEM_SPEC = pl.BlockSpec(memory_space=pltpu.VMEM)
SMEM_SPEC = pl.BlockSpec(memory_space=pltpu.SMEM)
ANY_SPEC = pl.BlockSpec(memory_space=pl.ANY)


def params(mebibytes):
    return pltpu.CompilerParams(vmem_limit_bytes=mebibytes << 20)


def whole_kernel(gram_ref, start_ref, basis_ref, inverse_ref):
    iterate(1.0, start_ref, basis_ref, gram_ref, inverse_ref)


def subspace_whole(gram, start):
    rank, order = start.shape
    return pl.pallas_call(
        whole_kernel,
        out_shape=jax.ShapeDtypeStruct((rank, order), jnp.float32),
        in_specs=[VMEM_SPEC] * 2,
        out_specs=VMEM_SPEC,
        scratch_shapes=[pltpu.VMEM((rank, rank), jnp.float32)],
        compiler_params=params(24),
        name="subspace_whole",
    )(gram, start)


def pieces_kernel(scale, place_ref, *refs):
    own_refs, cross_refs = refs[:8], refs[8:16]
    start_ref, basis_ref, gram_ref, packed_ref, inverse_ref, sems = refs[16:]
    x, y, core = place_ref[0], place_ref[1], place_ref[2]
    half = gram_ref.shape[0] // 2
    own_copies, cross_copies = [], []
    for index, (dc, dx, dy) in enumerate(PIECES):
        rows = own_refs[index].shape[0]
        at = pl.multiple_of(((core ^ dc) * 2 + (y ^ dy)) * rows, 8)
        own_copies.append(
            pltpu.make_async_copy(
                own_refs[index], packed_ref.at[x ^ dx, pl.ds(at, rows), :], sems.at[index]
            )
        )
        rows = cross_refs[index].shape[0]
        at = pl.multiple_of(((core ^ dc) * 4 + (x ^ dx) * 2 + (y ^ dy)) * rows, 8)
        cross_copies.append(
            pltpu.make_async_copy(
                cross_refs[index], gram_ref.at[pl.ds(at, rows), half:], sems.at[8 + index]
            )
        )
    for copy in own_copies + cross_copies:
        copy.start()
    for copy in own_copies:
        copy.wait()
    side = half // 4
    for p in range(2):
        at = [p * half + side * i for i in range(5)]
        last = packed_ref[p, :side, :]
        third = packed_ref[p, side : 2 * side, :]
        gram_ref[at[3] : at[4], at[0] : at[4]] = last
        gram_ref[at[0] : at[3], at[3] : at[4]] = last[:, : 3 * side].T
        gram_ref[at[2] : at[3], at[0] : at[3]] = third[:, : 3 * side]
        gram_ref[at[0] : at[2], at[2] : at[3]] = third[:, : 2 * side].T
        gram_ref[at[0] : at[1], at[0] : at[1]] = third[:, 3 * side :]
        second = packed_ref[p, 2 * side :, :]
        second = jnp.concatenate([second[:, : 2 * side], second[:, 2 * side :]], axis=0)
        gram_ref[at[1] : at[2], at[0] : at[2]] = second
        gram_ref[at[0] : at[1], at[1] : at[2]] = second[:, :side].T
    for copy in cross_copies:
        copy.wait()
    gram_ref[half:, :half] = gram_ref[:half, half:].T
    iterate(scale, start_ref, basis_ref, gram_ref, inverse_ref)


PIECES = [(dc, dx, dy) for dc in range(2) for dx, dy in ((0, 0), (1, 0), (0, 1), (1, 1))]


def subspace_pieces(place, own, cross, start, scale):
    rank, order = start.shape
    half = order // 2
    return pl.pallas_call(
        functools.partial(pieces_kernel, scale),
        out_shape=jax.ShapeDtypeStruct((rank, order), jnp.float32),
        in_specs=[SMEM_SPEC] + [ANY_SPEC] * 16 + [VMEM_SPEC],
        out_specs=VMEM_SPEC,
        scratch_shapes=[
            pltpu.VMEM((order, order), jnp.float32),
            pltpu.VMEM((2, 5 * half // 8, half), jnp.float32),
            pltpu.VMEM((rank, rank), jnp.float32),
            pltpu.SemaphoreType.DMA((16,)),
        ],
        compiler_params=params(16),
        name="subspace",
    )(place, *own, *cross, start)


def split(value):
    high = value.astype(jnp.bfloat16)
    return high, (value - high.astype(jnp.float32)).astype(jnp.bfloat16)


def dot3(left, right, contract):
    (a, b), (c, d) = left, right

    def dot(u, v):
        return lax.dot_general(u, v, (contract, ((), ())), preferred_element_type=jnp.float32)

    return dot(a, c) + (dot(a, d) + dot(b, c))


def pick(parts, rows):
    return parts[0][rows], parts[1][rows]


def own_kernel(place_ref, field_ref, keep_ref, send_ref, total_ref):
    half = field_ref.shape[2]
    side = half // 4
    values = split(jnp.concatenate([field_ref[s, 0] for s in range(field_ref.shape[0])], axis=1))

    @pl.when(pl.program_id(0) == 0)
    def _():
        total_ref[...] = jnp.zeros_like(total_ref)

    upper = dot3(pick(values, slice(0, 2 * side)), pick(values, slice(0, 2 * side)), NT)
    below = dot3(pick(values, slice(2 * side, half)), values, NT)
    total_ref[:side, :] += below[side:]
    total_ref[side : 2 * side, : 3 * side] += below[:side, : 3 * side]
    total_ref[side : 2 * side, 3 * side :] += upper[:side, :side]
    total_ref[2 * side :, : 2 * side] += upper[side : side + side // 2]
    total_ref[2 * side :, 2 * side :] += upper[side + side // 2 :]

    @pl.when(pl.program_id(0) == pl.num_programs(0) - 1)
    def _():
        rows = keep_ref.shape[0]
        core = place_ref[2]
        keep_ref[...] = total_ref[pl.ds(pl.multiple_of(core * rows, 8), rows), :]
        send_ref[...] = total_ref[pl.ds(pl.multiple_of((1 - core) * rows, 8), rows), :]


def own_blocks(place, field):
    half = field.shape[2]
    rows = 5 * half // 8
    step = math.gcd(field.shape[0], 4)
    shape = jax.ShapeDtypeStruct((rows // 2, half), jnp.float32)
    return pl.pallas_call(
        own_kernel,
        grid=(field.shape[0] // step,),
        out_shape=[shape, shape],
        in_specs=[SMEM_SPEC, pl.BlockSpec((step, 1, half, field.shape[3]), lambda i: (i, 0, 0, 0))],
        out_specs=[pl.BlockSpec((rows // 2, half), lambda i: (0, 0))] * 2,
        scratch_shapes=[pltpu.VMEM((rows, half), jnp.float32)],
        compiler_params=params(56),
        cost_estimate=pl.CostEstimate(flops=2 * 10**11, bytes_accessed=field.size * 4, transcendentals=0),
        name="own_blocks",
    )(place, field)


def species_pairs(refs):
    slots = [(i, s) for i, ref in enumerate(refs) for s in range(ref.shape[0])]
    return [slots[i : i + 2] for i in range(0, len(slots), 2)]


def cross_kernel(count, last, place_ref, *refs):
    got_refs, kept_refs = refs[:count], refs[count : 2 * count]
    refs = refs[2 * count :]
    x, core = place_ref[0], place_ref[2]
    half = got_refs[0].shape[2]
    rows = half // 2
    in_order = x == 0

    def product(at):
        total = None
        some, every = pl.ds(at, rows), slice(None)
        for pair in species_pairs(got_refs):
            def two(refs, where):
                return jnp.concatenate([refs[i][s, 0, where, :] for i, s in pair], axis=1)

            low = split(jnp.where(in_order, two(kept_refs, some), two(got_refs, some)))
            high = split(jnp.where(in_order, two(got_refs, every), two(kept_refs, every)))
            value = dot3(low, high, NT)
            total = value if total is None else total + value
        return total

    keep_at = pl.multiple_of(core * rows, 8)
    send_at = pl.multiple_of((1 - core) * rows, 8)
    if last:
        so_far_keep, so_far_send, keep_ref, send_ref = refs
        send_ref[...] = so_far_send[...] + product(send_at)
        keep_ref[...] = so_far_keep[...] + product(keep_at)
    else:
        keep_ref, send_ref = refs
        send_ref[...] = product(send_at)
        keep_ref[...] = product(keep_at)


def cross_block(place, got, kept, so_far):
    half = got[0].shape[2]
    shape = jax.ShapeDtypeStruct((half // 2, half), jnp.float32)
    return pl.pallas_call(
        functools.partial(cross_kernel, len(got), bool(so_far)),
        out_shape=[shape, shape],
        in_specs=[SMEM_SPEC] + [VMEM_SPEC] * (2 * len(got) + len(so_far)),
        out_specs=[VMEM_SPEC] * 2,
        compiler_params=params(24),
        name="cross_block",
    )(place, *got, *kept, *so_far)


def quarters_kernel(place_ref, left_ref, right_ref, *out_refs):
    rows = out_refs[0].shape[0]
    x, y = place_ref[0], place_ref[1]
    for ref, (dx, dy) in zip(out_refs, ((0, 0),) + CORNERS):
        some = pl.ds(pl.multiple_of(((x ^ dx) * 2 + (y ^ dy)) * rows, 8), rows)
        ref[...] = left_ref[some, :] + right_ref[some, :]


def sum_quarters(place, left, right):
    shape = jax.ShapeDtypeStruct((left.shape[0] // 4, left.shape[1]), jnp.float32)
    return pl.pallas_call(
        quarters_kernel,
        out_shape=[shape] * 4,
        in_specs=[SMEM_SPEC] + [VMEM_SPEC] * 2,
        out_specs=[VMEM_SPEC] * 4,
        compiler_params=params(24),
        name="quarters",
    )(place, left, right)


def project_kernel(count, place_ref, basis_ref, *refs):
    got_refs, kept_refs = refs[:count], refs[count : 2 * count]
    own_rows_ref, slab_refs, value_ref = refs[2 * count], refs[2 * count + 1 : -1], refs[-1]
    x, z, index = place_ref[0], place_ref[3], place_ref[4]
    half = got_refs[0].shape[2]
    width = got_refs[0].shape[3]
    near = split(basis_ref[:, pl.ds(pl.multiple_of(x * half, 128), half)])
    far = split(basis_ref[:, pl.ds(pl.multiple_of((1 - x) * half, 128), half)])
    slabs = len(slab_refs)
    rows = slab_refs[0].shape[2]
    for number, pair in enumerate(species_pairs(got_refs)):
        def two(refs):
            return split(jnp.concatenate([refs[i][s, 0] for i, s in pair], axis=1))

        value_ref[...] = dot3(near, two(kept_refs), NN) + dot3(far, two(got_refs), NN)
        for step in range(slabs):
            at = pl.multiple_of(lax.rem(z + step, slabs) * rows, 8)
            for j in range(len(pair)):
                slab_refs[step][2 * number + j, 0] = value_ref[
                    pl.ds(at, rows), width * j : width * (j + 1)
                ]
    count_rows = own_rows_ref.shape[0]
    per_tile = 128 // count_rows
    tile = basis_ref[:, pl.ds(pl.multiple_of(index // per_tile * 128, 128), 128)].T
    shift = lax.rem(index, per_tile)
    value_ref[:, :width] = tile
    own_rows_ref[...] = value_ref[pl.ds(pl.multiple_of(shift * count_rows, 8), count_rows), :width]


def project_slabs(place, basis, got, kept, slabs, own_rows):
    rank = basis.shape[0]
    species = sum(piece.shape[0] for piece in got)
    width = got[0].shape[3]
    slab = jax.ShapeDtypeStruct((species, 1, rank // slabs, width), jnp.float32)
    rows = jax.ShapeDtypeStruct((own_rows, rank), jnp.float32)
    return pl.pallas_call(
        functools.partial(project_kernel, len(got)),
        out_shape=[rows] + [slab] * slabs,
        in_specs=[SMEM_SPEC] + [VMEM_SPEC] * (1 + 2 * len(got)),
        out_specs=[VMEM_SPEC] * (1 + slabs),
        scratch_shapes=[pltpu.VMEM((rank, 2 * width), jnp.float32)],
        compiler_params=params(24),
        name="project",
    )(place, basis, *got, *kept)


def join_kernel(place_ref, *refs):
    out_ref = refs[-1]
    slabs = len(refs) - 1
    width = refs[0].shape[3]
    for step in range(slabs):
        source = lax.rem(place_ref[3] + slabs - step, slabs)
        out_ref[:, :, :, pl.ds(pl.multiple_of(source * width, 128), width)] = refs[step][...]


def join_slabs(place, slabs):
    shape = slabs[0].shape[:3] + (slabs[0].shape[3] * len(slabs),)
    return pl.pallas_call(
        join_kernel,
        out_shape=jax.ShapeDtypeStruct(shape, jnp.float32),
        in_specs=[SMEM_SPEC] + [VMEM_SPEC] * len(slabs),
        out_specs=VMEM_SPEC,
        compiler_params=params(24),
        name="join",
    )(place, *slabs)


def blocks(array, count):
    return array.reshape((count, array.shape[0] // count) + array.shape[1:])


def part(array, index):
    return lax.dynamic_index_in_dim(array, index, 0, keepdims=False)


def flip(size, bit):
    return [(i, i ^ bit) for i in range(size)]


def turn(size, step):
    return [(i, (i + step) % size) for i in range(size)]


def after(value, *others):
    return lax.optimization_barrier((value, others))[0]


def send_core(array):
    return lax.ppermute(array, "sa", flip(lax.axis_size("sa"), 1))


def send_corner(array, dx, dy):
    size = lax.axis_size("sa")
    pairs = [(x * size + s, (x ^ dx) * size + (s ^ (2 * dy))) for x in range(2) for s in range(size)]
    return lax.ppermute(array, ("gx", "sa"), pairs)


def sum_z(array, *others):
    size = lax.axis_size("gy")
    shares = [lax.ppermute(array, "gy", turn(size, step)) for step in range(1, size)]
    return sum(after(shares, others), array)


def gather_pieces(array):
    near = [array] + [send_corner(array, dx, dy) for dx, dy in CORNERS]
    return near + [send_core(piece) for piece in near]


def chunk_sizes(species):
    return [3, species - 5, 2]


def on_halves(field, start):
    x = lax.axis_index("gx")
    y = lax.axis_index("sa") // 2
    core = lax.axis_index("sa") % 2
    z = lax.axis_index("gy")
    place = jnp.stack([x, y, core, z, lax.axis_index(("gx", "gy", "sa"))]).astype(jnp.int32)
    species = field.shape[0] // 2
    columns = field.shape[0] * field.shape[1] * field.shape[3]
    columns = columns * lax.axis_size("gy") * lax.axis_size("sa")
    sizes = chunk_sizes(species)
    starts = [sum(sizes[:i]) for i in range(len(sizes))]

    def chunk(source, owner, i):
        return lax.dynamic_slice_in_dim(source, owner * species + starts[i], sizes[i], 0)

    sent = [chunk(field, 1 - x, 0)]
    rest = after(field, sent[0])
    sent = sent + [chunk(rest, 1 - x, i) for i in range(1, len(sizes))]
    got = [lax.ppermute(piece, "gx", flip(2, 1)) for piece in sent]

    own_field = after(rest, sent)
    own_keep, own_send = own_blocks(place, own_field)
    own = blocks(after(own_keep + send_core(own_send), got[0]), 2)
    own = part(own, y) + send_corner(part(own, 1 - y), 0, 1)
    kept = [chunk(own_field, x, i) for i in range(len(sizes))]
    start_t = start.T
    *early_got, final_got = got
    so_far = cross_block(place, early_got, kept[:-1], ())
    own = sum_z(own, so_far, kept, start_t)
    beside = send_corner(own, 0, 1)

    final_got = after(final_got, beside)
    cross_keep, cross_send = cross_block(place, [final_got], kept[-1:], so_far)
    cross, *shares = sum_quarters(place, cross_keep, send_core(cross_send))
    shares = [send_corner(share, dx, dy) for share, (dx, dy) in zip(shares, CORNERS)]
    own, beside = after((own, beside), shares[0])
    cross = sum(shares, cross)
    far, far_beside = send_corner(own, 1, 0), send_corner(beside, 1, 0)
    own_pieces = [own, far, beside, far_beside]
    own_pieces = own_pieces + [send_core(piece) for piece in own_pieces]
    cross_pieces = gather_pieces(sum_z(cross, far, far_beside))

    basis = subspace_pieces(place, own_pieces, cross_pieces, start_t, 1.0 / columns)
    devices = lax.axis_size(("gx", "gy", "sa"))
    slabs = lax.axis_size("gy")
    own_rows, *projected = project_slabs(
        place, basis, early_got + [final_got], kept, slabs, start.shape[0] // devices
    )
    arrived = [projected[0]] + [
        lax.ppermute(projected[i], "gy", turn(slabs, i)) for i in range(1, slabs)
    ]
    return join_slabs(place, arrived), own_rows


def outer(left, right):
    return jnp.einsum(
        "stxy,stzy->xz", left, right, precision=HIGH_PREC, preferred_element_type=jnp.float32
    )


def on_fibres(field, start):
    axes = ("gx", "gy", "sa")
    fibres = lax.all_to_all(field, "gx", split_axis=0, concat_axis=2, tiled=True)
    columns = fibres.shape[0] * fibres.shape[1] * fibres.shape[3] * lax.axis_size(axes)
    gram = lax.psum(outer(fibres, fibres), axes) / columns
    basis = subspace_whole(gram, start.T)
    projected = jnp.einsum(
        "kx,stxy->stky", basis, fibres, precision=HIGH_PREC, preferred_element_type=jnp.float32
    )
    rows_dev = start.shape[0] // lax.axis_size(axes)
    own_rows = lax.dynamic_slice_in_dim(basis.T, lax.axis_index(axes) * rows_dev, rows_dev, 0)
    return lax.all_to_all(projected, "gy", split_axis=2, concat_axis=3, tiled=True), own_rows


def on_device(scalar_field, start_basis):
    if lax.axis_size("gx") == 2 and lax.axis_size("sa") == 4:
        return on_halves(scalar_field, start_basis)
    return on_fibres(scalar_field, start_basis)


def solution(mesh):
    placed = (P("sa", None, "gx", "gy"), P())
    return jax.shard_map(
        on_device,
        mesh=mesh,
        in_specs=placed,
        out_specs=(P(("sa", "gx"), None, "gy", None), P(("gx", "gy", "sa"), None)),
        check_vma=False,
    )
```

```python
import functools
import math

import jax
import jax.numpy as jnp
from jax import lax
from jax.experimental import pallas as pl
from jax.experimental.pallas import tpu as pltpu
from jax.sharding import PartitionSpec as P

ITERS = 3
CORNERS = ((1, 0), (0, 1), (1, 1))
PANEL = 8
AHEAD = 3
SMALL = 1e-6
MEDIUM = 4e-4
NN = ((1,), (0,))
NT = ((1,), (1,))
HIGHEST_PREC = lax.Precision.HIGHEST
HIGH_PREC = lax.Precision.HIGH


def mul(left, right):
    return lax.dot_general(
        left, right, (((1,), (0,)), ((), ())), precision=HIGHEST_PREC, preferred_element_type=jnp.float32
    )


def mul_t(left, right):
    return lax.dot_general(
        left, right, (((1,), (1,)), ((), ())), precision=HIGHEST_PREC, preferred_element_type=jnp.float32
    )


def three_parts(value):
    high = value.astype(jnp.bfloat16)
    rest = value - high.astype(jnp.float32)
    middle = rest.astype(jnp.bfloat16)
    return high, middle, (rest - middle.astype(jnp.float32)).astype(jnp.bfloat16)


def inverse_factor(matrix):
    order = matrix.shape[0]
    panels = order // PANEL
    shape = (PANEL, order)
    sub = lax.broadcasted_iota(jnp.int32, shape, 0)
    lane = lax.broadcasted_iota(jnp.int32, shape, 1)
    rows = [matrix[PANEL * q : PANEL * (q + 1), :] for q in range(panels)]

    def spread(q, p):
        return [
            jnp.broadcast_to(rows[q][:, PANEL * p + j : PANEL * p + j + 1], shape) for j in range(PANEL)
        ]

    def sublane(value, k):
        return jnp.broadcast_to(value[k : k + 1, :], shape)

    following = spread(0, 0)
    for p in range(panels):
        near = list(range(p + 1, min(p + 1 + AHEAD, panels)))
        columns = {q: spread(q, p) for q in near}
        columns[p] = following
        following = spread(p + 1, p + 1) if near else []
        inside = (lane >= PANEL * p) & (lane < PANEL * (p + 1))
        rows[p] = jnp.where(inside, jnp.where(lane == sub + PANEL * p, 1.0, 0.0), rows[p])
        for q in range(p + 1, panels):
            rows[q] = jnp.where(inside, 0.0, rows[q])
        for j in range(PANEL):
            scale = lax.rsqrt(sublane(columns[p][j], j))
            factor = {q: columns[q][j] * scale for q in [p] + near}
            row = sublane(rows[p], j) * scale
            for k in range(j + 1, PANEL):
                pivot = sublane(factor[p], k)
                for q in [p] + near:
                    columns[q][k] = columns[q][k] - factor[q] * pivot
            for k in range(len(following)):
                following[k] = following[k] - factor[p + 1] * sublane(factor[p + 1], k)
            below = jnp.where(sub > j, factor[p], 0.0)
            rows[p] = jnp.where(sub == j, row, rows[p] - below * row)
            for q in near:
                rows[q] = rows[q] - factor[q] * row
        if p + 1 + AHEAD < panels:
            high, middle, low = (part.astype(jnp.float32) for part in three_parts(rows[p]))
            left = jnp.concatenate([high, high, high, middle, middle, low], axis=0)
            right = jnp.concatenate([high, middle, low, high, middle, high], axis=0)
            update = lax.dot_general(
                left.astype(jnp.bfloat16),
                right.astype(jnp.bfloat16),
                (((0,), (0,)), ((), ())),
                preferred_element_type=jnp.float32,
            )
            for q in range(p + 1 + AHEAD, panels):
                rows[q] = rows[q] - update[PANEL * q : PANEL * (q + 1), :]
    return jnp.concatenate(
        [jnp.where(lane <= sub + PANEL * q, rows[q], 0.0) for q in range(panels)], axis=0
    )


def lower(matrix, row, col):
    return jnp.where(row > col, matrix, jnp.where(row == col, 0.5 * matrix, 0.0))


def inverse_factor_near_one(error, row, col):
    first = lower(error, row, col)
    eye = jnp.where(row == col, 1.0, 0.0)
    return eye - first + (lower(mul_t(first, first), row, col) + mul(first, first))


def dot_t(left, right):
    return lax.dot_general(left, right, (NT, ((), ())), preferred_element_type=jnp.float32)


def inner_products(value):
    high, middle, low = three_parts(value)
    mixed = dot_t(high, middle) + dot_t(high, low)
    return dot_t(high, high) + ((mixed + mixed.T) + dot_t(middle, middle))


def apply(factor, value):
    a, b, c = three_parts(factor)
    high, middle, low = three_parts(value)

    def pass_of(left, right):
        return lax.dot_general(
            jnp.concatenate(left, axis=1),
            jnp.concatenate(right, axis=0),
            (NN, ((), ())),
            preferred_element_type=jnp.float32,
        )

    return pass_of([a, b], [high, middle]) + (
        pass_of([a, b], [middle, high]) + pass_of([a, c], [low, high])
    )


def iterate(scale, first_map, start_ref, basis_ref, gram_ref, inverse_ref, mapped_ref):
    rank = start_ref.shape[0]
    row = lax.broadcasted_iota(jnp.int32, (rank, rank), 0)
    col = lax.broadcasted_iota(jnp.int32, (rank, rank), 1)
    eye = jnp.where(row == col, 1.0, 0.0)
    basis_ref[...] = start_ref[...]

    def iteration(index, carry):
        @pl.when(index == 0)
        def _():
            first_map()

        @pl.when(index > 0)
        def _():
            mapped_ref[...] = mul(basis_ref[...], gram_ref[...])

        mapped = mapped_ref[...] * scale
        once = apply(inverse_factor(inner_products(mapped)), mapped)
        inner = inner_products(once)
        error = inner - eye
        size = jnp.sum(error * error)

        @pl.when(size <= MEDIUM)
        def _():
            inverse_ref[...] = inverse_factor_near_one(error, row, col)

        @pl.when(jnp.logical_and(size > SMALL, size <= MEDIUM))
        def _():
            about = inverse_ref[...]
            rest = mul_t(mul(about, inner), about) - eye
            inverse_ref[...] = about - mul(lower(rest, row, col), about)

        @pl.when(jnp.logical_not(size <= MEDIUM))
        def _():
            inverse_ref[...] = inverse_factor(inner)

        basis_ref[...] = apply(inverse_ref[...], once)
        return carry

    lax.fori_loop(0, ITERS, iteration, 0)


VMEM_SPEC = pl.BlockSpec(memory_space=pltpu.VMEM)
SMEM_SPEC = pl.BlockSpec(memory_space=pltpu.SMEM)
ANY_SPEC = pl.BlockSpec(memory_space=pl.ANY)


def params(mebibytes):
    return pltpu.CompilerParams(vmem_limit_bytes=mebibytes << 20)


def whole_kernel(gram_ref, start_ref, basis_ref, inverse_ref, mapped_ref):
    def first_map():
        mapped_ref[...] = mul(start_ref[...], gram_ref[...])

    iterate(1.0, first_map, start_ref, basis_ref, gram_ref, inverse_ref, mapped_ref)


def subspace_whole(gram, start):
    rank, order = start.shape
    return pl.pallas_call(
        whole_kernel,
        out_shape=jax.ShapeDtypeStruct((rank, order), jnp.float32),
        in_specs=[VMEM_SPEC] * 2,
        out_specs=VMEM_SPEC,
        scratch_shapes=[pltpu.VMEM((rank, rank), jnp.float32), pltpu.VMEM((rank, order), jnp.float32)],
        compiler_params=params(24),
        name="subspace_whole",
    )(gram, start)


def diagonal_kernel(place_ref, *refs):
    own_refs, (start_ref, gram_ref, head_ref, packed_ref) = refs[:8], refs[8:]
    x, y, core = place_ref[0], place_ref[1], place_ref[2]
    half = gram_ref.shape[1]
    side = half // 4
    for ref, (dc, dx, dy) in zip(own_refs, PIECES):
        rows = ref.shape[0]
        at = pl.multiple_of(((core ^ dc) * 2 + (y ^ dy)) * rows, 8)
        packed_ref[x ^ dx, pl.ds(at, rows), :] = ref[...]
    at = [side * i for i in range(5)]
    for p in range(2):
        last = packed_ref[p, :side, :]
        third = packed_ref[p, side : 2 * side, :]
        gram_ref[p, at[3] : at[4], at[0] : at[4]] = last
        gram_ref[p, at[0] : at[3], at[3] : at[4]] = last[:, : 3 * side].T
        gram_ref[p, at[2] : at[3], at[0] : at[3]] = third[:, : 3 * side]
        gram_ref[p, at[0] : at[2], at[2] : at[3]] = third[:, : 2 * side].T
        gram_ref[p, at[0] : at[1], at[0] : at[1]] = third[:, 3 * side :]
        second = packed_ref[p, 2 * side :, :]
        second = jnp.concatenate([second[:, : 2 * side], second[:, 2 * side :]], axis=0)
        gram_ref[p, at[1] : at[2], at[0] : at[2]] = second
        gram_ref[p, at[0] : at[1], at[1] : at[2]] = second[:, :side].T
        columns = slice(half * p, half * (p + 1))
        head_ref[:, columns] = mul(start_ref[:, columns], gram_ref[p])


def diagonal_blocks(place, own, start):
    rank, order = start.shape
    half = order // 2
    return pl.pallas_call(
        diagonal_kernel,
        out_shape=[
            jax.ShapeDtypeStruct((2, half, half), jnp.float32),
            jax.ShapeDtypeStruct((rank, order), jnp.float32),
        ],
        in_specs=[SMEM_SPEC] + [VMEM_SPEC] * 9,
        out_specs=[VMEM_SPEC] * 2,
        scratch_shapes=[pltpu.VMEM((2, 5 * half // 8, half), jnp.float32)],
        compiler_params=params(16),
        name="diagonal",
    )(place, *own, start)


def pieces_kernel(scale, count, place_ref, *refs):
    diagonal_ref, head_ref, start_ref, refs = refs[0], refs[1], refs[2], refs[3:]
    cross_refs, refs = refs[:8], refs[8:]
    kept_refs, got_refs, refs = refs[:count], refs[count : 2 * count], refs[2 * count :]
    own_rows_ref, *slab_refs = refs[:-8]
    basis_ref, gram_ref, mapped_ref, inverse_ref, fields_ref, value_ref, sems, field_sems = refs[-8:]
    x, y, core = place_ref[0], place_ref[1], place_ref[2]
    half = gram_ref.shape[0] // 2
    cross_copies, later_copies = [], []
    for index, (dc, dx, dy) in enumerate(PIECES):
        rows = cross_refs[index].shape[0]
        at = pl.multiple_of(((core ^ dc) * 4 + (x ^ dx) * 2 + (y ^ dy)) * rows, 8)
        cross_copies.append(
            pltpu.make_async_copy(
                cross_refs[index], gram_ref.at[pl.ds(at, rows), half:], sems.at[index]
            )
        )
    for p in range(2):
        square = pl.ds(half * p, half)
        later_copies.append(
            pltpu.make_async_copy(diagonal_ref.at[p], gram_ref.at[square, square], sems.at[8 + p])
        )
    for side, sources in enumerate((kept_refs, got_refs)):
        first = 0
        for index, ref in enumerate(sources):
            later_copies.append(
                pltpu.make_async_copy(
                    ref.at[:, 0],
                    fields_ref.at[side, first : first + ref.shape[0]],
                    field_sems.at[side, index],
                )
            )
            first += ref.shape[0]
    for copy in cross_copies + later_copies:
        copy.start()
    for copy in cross_copies:
        copy.wait()
    gram_ref[half:, :half] = gram_ref[:half, half:].T

    def first_map():
        mapped_ref[:, :half] = head_ref[:, :half] + mul(start_ref[:, half:], gram_ref[half:, :half])
        mapped_ref[:, half:] = head_ref[:, half:] + mul(start_ref[:, :half], gram_ref[:half, half:])
        for copy in later_copies:
            copy.wait()

    iterate(scale, first_map, start_ref, basis_ref, gram_ref, inverse_ref, mapped_ref)
    project(place_ref, basis_ref, fields_ref, own_rows_ref, slab_refs, value_ref)


PIECES = [(dc, dx, dy) for dc in range(2) for dx, dy in ((0, 0), (1, 0), (0, 1), (1, 1))]


def subspace_pieces(place, diagonal, head, start, cross, kept, got, scale, slabs, own_rows):
    rank, order = start.shape
    half = order // 2
    species = sum(piece.shape[0] for piece in got)
    width = got[0].shape[3]
    slab = jax.ShapeDtypeStruct((species, 1, rank // slabs, width), jnp.float32)
    return pl.pallas_call(
        functools.partial(pieces_kernel, scale, len(got)),
        out_shape=[jax.ShapeDtypeStruct((own_rows, rank), jnp.float32)] + [slab] * slabs,
        in_specs=[SMEM_SPEC, ANY_SPEC] + [VMEM_SPEC] * 2 + [ANY_SPEC] * (8 + 2 * len(got)),
        out_specs=[VMEM_SPEC] * (1 + slabs),
        scratch_shapes=[
            pltpu.VMEM((rank, order), jnp.float32),
            pltpu.VMEM((order, order), jnp.float32),
            pltpu.VMEM((rank, order), jnp.float32),
            pltpu.VMEM((rank, rank), jnp.float32),
            pltpu.VMEM((2, species, half, width), jnp.float32),
            pltpu.VMEM((rank, 2 * width), jnp.float32),
            pltpu.SemaphoreType.DMA((10,)),
            pltpu.SemaphoreType.DMA((2, len(got))),
        ],
        compiler_params=params(24),
        name="subspace",
    )(place, diagonal, head, start, *cross, *kept, *got)


def split(value):
    high = value.astype(jnp.bfloat16)
    return high, (value - high.astype(jnp.float32)).astype(jnp.bfloat16)


def dot3(left, right, contract):
    (a, b), (c, d) = left, right

    def dot(u, v):
        return lax.dot_general(u, v, (contract, ((), ())), preferred_element_type=jnp.float32)

    return dot(a, c) + (dot(a, d) + dot(b, c))


def pick(parts, rows):
    return parts[0][rows], parts[1][rows]


def project(place_ref, basis_ref, fields_ref, own_rows_ref, slab_refs, value_ref):
    x, z, index = place_ref[0], place_ref[3], place_ref[4]
    species, half, width = fields_ref.shape[1:]
    near = split(basis_ref[:, pl.ds(pl.multiple_of(x * half, 128), half)])
    far = split(basis_ref[:, pl.ds(pl.multiple_of((1 - x) * half, 128), half)])
    slabs = len(slab_refs)
    rows = slab_refs[0].shape[2]
    for first in range(0, species, 2):

        def two(side):
            return split(jnp.concatenate([fields_ref[side, first], fields_ref[side, first + 1]], axis=1))

        value_ref[...] = dot3(near, two(0), NN) + dot3(far, two(1), NN)
        for step in range(slabs):
            at = pl.multiple_of(lax.rem(z + step, slabs) * rows, 8)
            for j in range(2):
                slab_refs[step][first + j, 0] = value_ref[
                    pl.ds(at, rows), width * j : width * (j + 1)
                ]
    count_rows = own_rows_ref.shape[0]
    per_tile = 128 // count_rows
    tile = basis_ref[:, pl.ds(pl.multiple_of(index // per_tile * 128, 128), 128)].T
    shift = lax.rem(index, per_tile)
    value_ref[:, :width] = tile
    own_rows_ref[...] = value_ref[pl.ds(pl.multiple_of(shift * count_rows, 8), count_rows), :width]


def own_kernel(place_ref, field_ref, keep_ref, send_ref, total_ref):
    half = field_ref.shape[2]
    side = half // 4
    values = split(jnp.concatenate([field_ref[s, 0] for s in range(field_ref.shape[0])], axis=1))

    @pl.when(pl.program_id(0) == 0)
    def _():
        total_ref[...] = jnp.zeros_like(total_ref)

    upper = dot3(pick(values, slice(0, 2 * side)), pick(values, slice(0, 2 * side)), NT)
    below = dot3(pick(values, slice(2 * side, half)), values, NT)
    total_ref[:side, :] += below[side:]
    total_ref[side : 2 * side, : 3 * side] += below[:side, : 3 * side]
    total_ref[side : 2 * side, 3 * side :] += upper[:side, :side]
    total_ref[2 * side :, : 2 * side] += upper[side : side + side // 2]
    total_ref[2 * side :, 2 * side :] += upper[side + side // 2 :]

    @pl.when(pl.program_id(0) == pl.num_programs(0) - 1)
    def _():
        rows = keep_ref.shape[0]
        core = place_ref[2]
        keep_ref[...] = total_ref[pl.ds(pl.multiple_of(core * rows, 8), rows), :]
        send_ref[...] = total_ref[pl.ds(pl.multiple_of((1 - core) * rows, 8), rows), :]


def own_blocks(place, field):
    half = field.shape[2]
    rows = 5 * half // 8
    step = math.gcd(field.shape[0], 4)
    shape = jax.ShapeDtypeStruct((rows // 2, half), jnp.float32)
    return pl.pallas_call(
        own_kernel,
        grid=(field.shape[0] // step,),
        out_shape=[shape, shape],
        in_specs=[SMEM_SPEC, pl.BlockSpec((step, 1, half, field.shape[3]), lambda i: (i, 0, 0, 0))],
        out_specs=[pl.BlockSpec((rows // 2, half), lambda i: (0, 0))] * 2,
        scratch_shapes=[pltpu.VMEM((rows, half), jnp.float32)],
        compiler_params=params(56),
        cost_estimate=pl.CostEstimate(flops=2 * 10**11, bytes_accessed=field.size * 4, transcendentals=0),
        name="own_blocks",
    )(place, field)


def species_pairs(refs):
    slots = [(i, s) for i, ref in enumerate(refs) for s in range(ref.shape[0])]
    return [slots[i : i + 2] for i in range(0, len(slots), 2)]


def cross_kernel(count, last, halves, place_ref, *refs):
    got_refs, kept_refs = refs[:count], refs[count : 2 * count]
    refs = refs[2 * count :]
    x, core = place_ref[0], place_ref[2]
    half = got_refs[0].shape[2]
    rows = half // 2
    in_order = x == 0

    def product(at):
        total = None
        some, every = pl.ds(at, rows), slice(None)
        for pair in species_pairs(got_refs):
            def two(refs, where):
                return jnp.concatenate([refs[i][s, 0, where, :] for i, s in pair], axis=1)

            low = split(jnp.where(in_order, two(kept_refs, some), two(got_refs, some)))
            high = split(jnp.where(in_order, two(got_refs, every), two(kept_refs, every)))
            value = dot3(low, high, NT)
            total = value if total is None else total + value
        return total

    for name, so_far, out in zip(halves, refs, refs[-len(halves) :]):
        at = pl.multiple_of((core if name == "keep" else 1 - core) * rows, 8)
        out[...] = product(at) + so_far[...] if last else product(at)


def cross_block(place, got, kept, halves, so_far=()):
    half = got[0].shape[2]
    shape = jax.ShapeDtypeStruct((half // 2, half), jnp.float32)
    return pl.pallas_call(
        functools.partial(cross_kernel, len(got), bool(so_far), halves),
        out_shape=[shape] * len(halves),
        in_specs=[SMEM_SPEC] + [VMEM_SPEC] * (2 * len(got) + len(so_far)),
        out_specs=[VMEM_SPEC] * len(halves),
        compiler_params=params(24),
        name="cross_block",
    )(place, *got, *kept, *so_far)


def quarters_kernel(place_ref, left_ref, right_ref, *out_refs):
    rows = out_refs[0].shape[0]
    x, y = place_ref[0], place_ref[1]
    for ref, (dx, dy) in zip(out_refs, ((0, 0),) + CORNERS):
        some = pl.ds(pl.multiple_of(((x ^ dx) * 2 + (y ^ dy)) * rows, 8), rows)
        ref[...] = left_ref[some, :] + right_ref[some, :]


def sum_quarters(place, left, right):
    shape = jax.ShapeDtypeStruct((left.shape[0] // 4, left.shape[1]), jnp.float32)
    return pl.pallas_call(
        quarters_kernel,
        out_shape=[shape] * 4,
        in_specs=[SMEM_SPEC] + [VMEM_SPEC] * 2,
        out_specs=[VMEM_SPEC] * 4,
        compiler_params=params(24),
        name="quarters",
    )(place, left, right)


def join_kernel(place_ref, *refs):
    out_ref = refs[-1]
    slabs = len(refs) - 1
    width = refs[0].shape[3]
    for step in range(slabs):
        source = lax.rem(place_ref[3] + slabs - step, slabs)
        out_ref[:, :, :, pl.ds(pl.multiple_of(source * width, 128), width)] = refs[step][...]


def join_slabs(place, slabs):
    shape = slabs[0].shape[:3] + (slabs[0].shape[3] * len(slabs),)
    return pl.pallas_call(
        join_kernel,
        out_shape=jax.ShapeDtypeStruct(shape, jnp.float32),
        in_specs=[SMEM_SPEC] + [VMEM_SPEC] * len(slabs),
        out_specs=VMEM_SPEC,
        compiler_params=params(24),
        name="join",
    )(place, *slabs)


def blocks(array, count):
    return array.reshape((count, array.shape[0] // count) + array.shape[1:])


def part(array, index):
    return lax.dynamic_index_in_dim(array, index, 0, keepdims=False)


def flip(size, bit):
    return [(i, i ^ bit) for i in range(size)]


def turn(size, step):
    return [(i, (i + step) % size) for i in range(size)]


def after(value, *others):
    return lax.optimization_barrier((value, others))[0]


def send_core(array):
    return lax.ppermute(array, "sa", flip(lax.axis_size("sa"), 1))


def send_corner(array, dx, dy):
    size = lax.axis_size("sa")
    pairs = [(x * size + s, (x ^ dx) * size + (s ^ (2 * dy))) for x in range(2) for s in range(size)]
    return lax.ppermute(array, ("gx", "sa"), pairs)


def sum_z(array, *others):
    size = lax.axis_size("gy")
    shares = [lax.ppermute(array, "gy", turn(size, step)) for step in range(1, size)]
    return sum(after(shares, others), array)


def chunk_sizes(species):
    return [3, species - 5, 2]


def on_halves(field, start):
    x = lax.axis_index("gx")
    y = lax.axis_index("sa") // 2
    core = lax.axis_index("sa") % 2
    z = lax.axis_index("gy")
    place = jnp.stack([x, y, core, z, lax.axis_index(("gx", "gy", "sa"))]).astype(jnp.int32)
    species = field.shape[0] // 2
    columns = field.shape[0] * field.shape[1] * field.shape[3]
    columns = columns * lax.axis_size("gy") * lax.axis_size("sa")
    sizes = chunk_sizes(species)
    starts = [sum(sizes[:i]) for i in range(len(sizes))]

    def chunk(source, owner, i):
        return lax.dynamic_slice_in_dim(source, owner * species + starts[i], sizes[i], 0)

    sent = [chunk(field, 1 - x, 0)]
    rest = after(field, sent[0])
    sent = sent + [chunk(rest, 1 - x, i) for i in range(1, len(sizes))]
    got = [lax.ppermute(piece, "gx", flip(2, 1)) for piece in sent]

    own_field = after(rest, sent)
    own_keep, own_send = own_blocks(place, own_field)
    own = blocks(after(own_keep + send_core(own_send), got[0]), 2)
    own = part(own, y) + send_corner(part(own, 1 - y), 0, 1)
    kept = [chunk(own_field, x, i) for i in range(len(sizes))]
    start_t = start.T
    *early_got, final_got = got
    so_far_send, so_far_keep = cross_block(place, early_got, kept[:-1], ("send", "keep"))
    own = sum_z(own, so_far_send, so_far_keep, kept, start_t)
    beside = send_corner(own, 0, 1)

    final_got = after(final_got, own)
    (cross_send,) = cross_block(place, [final_got], kept[-1:], ("send",), (so_far_send,))
    cross_sent = send_core(after(cross_send, beside))
    (cross_keep,) = cross_block(
        place, [final_got], kept[-1:], ("keep",), (after(so_far_keep, cross_send),)
    )
    cross, *shares = sum_quarters(place, cross_keep, cross_sent)
    shares = [send_corner(share, dx, dy) for share, (dx, dy) in zip(shares, CORNERS)]
    own, beside = after((own, beside), shares[0])
    cross = sum(shares, cross)
    own_pieces = [own, send_corner(own, 1, 0), beside, send_corner(beside, 1, 0)]
    own_pieces = own_pieces + [send_core(piece) for piece in own_pieces]
    cross = sum_z(cross, own_pieces[:4])
    diagonal, head = diagonal_blocks(place, own_pieces, start_t)
    near = [cross] + [send_corner(cross, dx, dy) for dx, dy in CORNERS]
    cross_pieces = near + [send_core(after(piece, head)) for piece in near]

    slabs = lax.axis_size("gy")
    own_rows, *projected = subspace_pieces(
        place,
        diagonal,
        head,
        start_t,
        cross_pieces,
        kept,
        early_got + [final_got],
        1.0 / columns,
        slabs,
        start.shape[0] // lax.axis_size(("gx", "gy", "sa")),
    )
    arrived = [projected[0]] + [
        lax.ppermute(projected[i], "gy", turn(slabs, i)) for i in range(1, slabs)
    ]
    return join_slabs(place, arrived), own_rows


def outer(left, right):
    return jnp.einsum(
        "stxy,stzy->xz", left, right, precision=HIGH_PREC, preferred_element_type=jnp.float32
    )


def on_fibres(field, start):
    axes = ("gx", "gy", "sa")
    fibres = lax.all_to_all(field, "gx", split_axis=0, concat_axis=2, tiled=True)
    columns = fibres.shape[0] * fibres.shape[1] * fibres.shape[3] * lax.axis_size(axes)
    gram = lax.psum(outer(fibres, fibres), axes) / columns
    basis = subspace_whole(gram, start.T)
    projected = jnp.einsum(
        "kx,stxy->stky", basis, fibres, precision=HIGH_PREC, preferred_element_type=jnp.float32
    )
    rows_dev = start.shape[0] // lax.axis_size(axes)
    own_rows = lax.dynamic_slice_in_dim(basis.T, lax.axis_index(axes) * rows_dev, rows_dev, 0)
    return lax.all_to_all(projected, "gy", split_axis=2, concat_axis=3, tiled=True), own_rows


def on_device(scalar_field, start_basis):
    if lax.axis_size("gx") == 2 and lax.axis_size("sa") == 4:
        return on_halves(scalar_field, start_basis)
    return on_fibres(scalar_field, start_basis)


def solution(mesh):
    placed = (P("sa", None, "gx", "gy"), P())
    return jax.shard_map(
        on_device,
        mesh=mesh,
        in_specs=placed,
        out_specs=(P(("sa", "gx"), None, "gy", None), P(("gx", "gy", "sa"), None)),
        check_vma=False,
    )
```

```python
import functools
import math

import jax
import jax.numpy as jnp
from jax import lax
from jax.experimental import pallas as pl
from jax.experimental.pallas import tpu as pltpu
from jax.sharding import PartitionSpec as P

ITERS = 3
CORNERS = ((1, 0), (0, 1), (1, 1))
PANEL = 8
AHEAD = 3
SMALL = 1e-4
MEDIUM = 4e-4
NN = ((1,), (0,))
NT = ((1,), (1,))
HIGHEST_PREC = lax.Precision.HIGHEST
HIGH_PREC = lax.Precision.HIGH


def mul(left, right):
    return lax.dot_general(
        left, right, (((1,), (0,)), ((), ())), precision=HIGHEST_PREC, preferred_element_type=jnp.float32
    )


def mul_t(left, right):
    return lax.dot_general(
        left, right, (((1,), (1,)), ((), ())), precision=HIGHEST_PREC, preferred_element_type=jnp.float32
    )


def three_parts(value):
    high = value.astype(jnp.bfloat16)
    rest = value - high.astype(jnp.float32)
    middle = rest.astype(jnp.bfloat16)
    return high, middle, (rest - middle.astype(jnp.float32)).astype(jnp.bfloat16)


def inverse_factor(matrix):
    order = matrix.shape[0]
    panels = order // PANEL
    shape = (PANEL, order)
    sub = lax.broadcasted_iota(jnp.int32, shape, 0)
    lane = lax.broadcasted_iota(jnp.int32, shape, 1)
    rows = [matrix[PANEL * q : PANEL * (q + 1), :] for q in range(panels)]

    def spread(q, p):
        return [
            jnp.broadcast_to(rows[q][:, PANEL * p + j : PANEL * p + j + 1], shape) for j in range(PANEL)
        ]

    def sublane(value, k):
        return jnp.broadcast_to(value[k : k + 1, :], shape)

    following = spread(0, 0)
    for p in range(panels):
        near = list(range(p + 1, min(p + 1 + AHEAD, panels)))
        columns = {q: spread(q, p) for q in near}
        columns[p] = following
        following = spread(p + 1, p + 1) if near else []
        inside = (lane >= PANEL * p) & (lane < PANEL * (p + 1))
        rows[p] = jnp.where(inside, jnp.where(lane == sub + PANEL * p, 1.0, 0.0), rows[p])
        for q in range(p + 1, panels):
            rows[q] = jnp.where(inside, 0.0, rows[q])
        for j in range(PANEL):
            scale = lax.rsqrt(sublane(columns[p][j], j))
            factor = {q: columns[q][j] * scale for q in [p] + near}
            row = sublane(rows[p], j) * scale
            for k in range(j + 1, PANEL):
                pivot = sublane(factor[p], k)
                for q in [p] + near:
                    columns[q][k] = columns[q][k] - factor[q] * pivot
            for k in range(len(following)):
                following[k] = following[k] - factor[p + 1] * sublane(factor[p + 1], k)
            below = jnp.where(sub > j, factor[p], 0.0)
            rows[p] = jnp.where(sub == j, row, rows[p] - below * row)
            for q in near:
                rows[q] = rows[q] - factor[q] * row
        if p + 1 + AHEAD < panels:
            high, middle, low = (part.astype(jnp.float32) for part in three_parts(rows[p]))
            left = jnp.concatenate([high, high, high, middle, middle, low], axis=0)
            right = jnp.concatenate([high, middle, low, high, middle, high], axis=0)
            update = lax.dot_general(
                left.astype(jnp.bfloat16),
                right.astype(jnp.bfloat16),
                (((0,), (0,)), ((), ())),
                preferred_element_type=jnp.float32,
            )
            for q in range(p + 1 + AHEAD, panels):
                rows[q] = rows[q] - update[PANEL * q : PANEL * (q + 1), :]
    return jnp.concatenate(
        [jnp.where(lane <= sub + PANEL * q, rows[q], 0.0) for q in range(panels)], axis=0
    )


def lower(matrix, row, col):
    return jnp.where(row > col, matrix, jnp.where(row == col, 0.5 * matrix, 0.0))


def inverse_factor_near_one(error, row, col):
    first = lower(error, row, col)
    eye = jnp.where(row == col, 1.0, 0.0)
    part = first.astype(jnp.bfloat16)
    square = lax.dot_general(part, part, (NN, ((), ())), preferred_element_type=jnp.float32)
    return eye - first + (lower(dot_t(part, part), row, col) + square)


def dot_t(left, right):
    return lax.dot_general(left, right, (NT, ((), ())), preferred_element_type=jnp.float32)


def inner_products(value):
    high, middle, low = three_parts(value)
    mixed = dot_t(high, middle) + dot_t(high, low)
    return dot_t(high, high) + ((mixed + mixed.T) + dot_t(middle, middle))


def apply(factor, value):
    a, b, c = three_parts(factor)
    high, middle, low = three_parts(value)

    def pass_of(left, right):
        return lax.dot_general(
            jnp.concatenate(left, axis=1),
            jnp.concatenate(right, axis=0),
            (NN, ((), ())),
            preferred_element_type=jnp.float32,
        )

    return pass_of([a, b], [high, middle]) + (
        pass_of([a, b], [middle, high]) + pass_of([a, c], [low, high])
    )


def iterate(scale, first_map, start_ref, basis_ref, gram_ref, inverse_ref, mapped_ref):
    rank = start_ref.shape[0]
    row = lax.broadcasted_iota(jnp.int32, (rank, rank), 0)
    col = lax.broadcasted_iota(jnp.int32, (rank, rank), 1)
    eye = jnp.where(row == col, 1.0, 0.0)
    basis_ref[...] = start_ref[...]

    def iteration(index, carry):
        @pl.when(index == 0)
        def _():
            first_map()

        @pl.when(index > 0)
        def _():
            mapped_ref[...] = mul(basis_ref[...], gram_ref[...])

        mapped = mapped_ref[...] * scale
        once = apply(inverse_factor(inner_products(mapped)), mapped)
        inner = inner_products(once)
        error = inner - eye
        size = jnp.sum(error * error)

        @pl.when(size <= MEDIUM)
        def _():
            inverse_ref[...] = inverse_factor_near_one(error, row, col)

        @pl.when(jnp.logical_and(size > SMALL, size <= MEDIUM))
        def _():
            about = inverse_ref[...]
            rest = mul_t(mul(about, inner), about) - eye
            inverse_ref[...] = about - mul(lower(rest, row, col), about)

        @pl.when(jnp.logical_not(size <= MEDIUM))
        def _():
            inverse_ref[...] = inverse_factor(inner)

        basis_ref[...] = apply(inverse_ref[...], once)
        return carry

    lax.fori_loop(0, ITERS, iteration, 0)


VMEM_SPEC = pl.BlockSpec(memory_space=pltpu.VMEM)
SMEM_SPEC = pl.BlockSpec(memory_space=pltpu.SMEM)
ANY_SPEC = pl.BlockSpec(memory_space=pl.ANY)


def params(mebibytes):
    return pltpu.CompilerParams(vmem_limit_bytes=mebibytes << 20)


def whole_kernel(gram_ref, start_ref, basis_ref, inverse_ref, mapped_ref):
    def first_map():
        mapped_ref[...] = mul(start_ref[...], gram_ref[...])

    iterate(1.0, first_map, start_ref, basis_ref, gram_ref, inverse_ref, mapped_ref)


def subspace_whole(gram, start):
    rank, order = start.shape
    return pl.pallas_call(
        whole_kernel,
        out_shape=jax.ShapeDtypeStruct((rank, order), jnp.float32),
        in_specs=[VMEM_SPEC] * 2,
        out_specs=VMEM_SPEC,
        scratch_shapes=[pltpu.VMEM((rank, rank), jnp.float32), pltpu.VMEM((rank, order), jnp.float32)],
        compiler_params=params(24),
        name="subspace_whole",
    )(gram, start)


def diagonal_kernel(place_ref, *refs):
    own_refs, (start_ref, gram_ref, head_ref, packed_ref) = refs[:8], refs[8:]
    x, y, core = place_ref[0], place_ref[1], place_ref[2]
    half = gram_ref.shape[1]
    side = half // 4
    for ref, (dc, dx, dy) in zip(own_refs, PIECES):
        rows = ref.shape[0]
        at = pl.multiple_of(((core ^ dc) * 2 + (y ^ dy)) * rows, 8)
        packed_ref[x ^ dx, pl.ds(at, rows), :] = ref[...]
    at = [side * i for i in range(5)]
    for p in range(2):
        last = packed_ref[p, :side, :]
        third = packed_ref[p, side : 2 * side, :]
        gram_ref[p, at[3] : at[4], at[0] : at[4]] = last
        gram_ref[p, at[0] : at[3], at[3] : at[4]] = last[:, : 3 * side].T
        gram_ref[p, at[2] : at[3], at[0] : at[3]] = third[:, : 3 * side]
        gram_ref[p, at[0] : at[2], at[2] : at[3]] = third[:, : 2 * side].T
        gram_ref[p, at[0] : at[1], at[0] : at[1]] = third[:, 3 * side :]
        second = packed_ref[p, 2 * side :, :]
        second = jnp.concatenate([second[:, : 2 * side], second[:, 2 * side :]], axis=0)
        gram_ref[p, at[1] : at[2], at[0] : at[2]] = second
        gram_ref[p, at[0] : at[1], at[1] : at[2]] = second[:, :side].T
        columns = slice(half * p, half * (p + 1))
        head_ref[:, columns] = mul(start_ref[:, columns], gram_ref[p])


def diagonal_blocks(place, own, start):
    rank, order = start.shape
    half = order // 2
    return pl.pallas_call(
        diagonal_kernel,
        out_shape=[
            jax.ShapeDtypeStruct((2, half, half), jnp.float32),
            jax.ShapeDtypeStruct((rank, order), jnp.float32),
        ],
        in_specs=[SMEM_SPEC] + [VMEM_SPEC] * 9,
        out_specs=[VMEM_SPEC] * 2,
        scratch_shapes=[pltpu.VMEM((2, 5 * half // 8, half), jnp.float32)],
        compiler_params=params(16),
        name="diagonal",
    )(place, *own, start)


def pieces_kernel(scale, place_ref, *refs):
    diagonal_ref, head_ref, start_ref, refs = refs[0], refs[1], refs[2], refs[3:]
    cross_refs, refs = refs[:8], refs[8:]
    field_refs, refs = refs[:2], refs[2:]
    own_rows_ref, *slab_refs = refs[:-8]
    basis_ref, gram_ref, mapped_ref, inverse_ref, high_ref, low_ref, value_ref, sems = refs[-8:]
    x, y, core = place_ref[0], place_ref[1], place_ref[2]
    half = gram_ref.shape[0] // 2
    cross_copies, later_copies = [], []
    for index, (dc, dx, dy) in enumerate(PIECES):
        rows = cross_refs[index].shape[0]
        at = pl.multiple_of(((core ^ dc) * 4 + (x ^ dx) * 2 + (y ^ dy)) * rows, 8)
        cross_copies.append(
            pltpu.make_async_copy(
                cross_refs[index], gram_ref.at[pl.ds(at, rows), half:], sems.at[index]
            )
        )
    for p in range(2):
        square = pl.ds(half * p, half)
        later_copies.append(
            pltpu.make_async_copy(diagonal_ref.at[p], gram_ref.at[square, square], sems.at[8 + p])
        )
    for index, (source, target) in enumerate(zip(field_refs, (high_ref, low_ref))):
        later_copies.append(pltpu.make_async_copy(source, target, sems.at[10 + index]))
    for copy in cross_copies + later_copies:
        copy.start()
    for copy in cross_copies:
        copy.wait()
    gram_ref[half:, :half] = gram_ref[:half, half:].T

    def first_map():
        mapped_ref[:, :half] = head_ref[:, :half] + mul(start_ref[:, half:], gram_ref[half:, :half])
        mapped_ref[:, half:] = head_ref[:, half:] + mul(start_ref[:, :half], gram_ref[:half, half:])
        for copy in later_copies:
            copy.wait()

    iterate(scale, first_map, start_ref, basis_ref, gram_ref, inverse_ref, mapped_ref)
    project(place_ref, basis_ref, high_ref, low_ref, own_rows_ref, slab_refs, value_ref)


PIECES = [(dc, dx, dy) for dc in range(2) for dx, dy in ((0, 0), (1, 0), (0, 1), (1, 1))]


def subspace_pieces(place, diagonal, head, start, cross, fields, scale, slabs, own_rows):
    rank, order = start.shape
    pairs, _, width = fields[0].shape
    slab = jax.ShapeDtypeStruct((2 * pairs, 1, rank // slabs, width // 2), jnp.float32)
    return pl.pallas_call(
        functools.partial(pieces_kernel, scale),
        out_shape=[jax.ShapeDtypeStruct((own_rows, rank), jnp.float32)] + [slab] * slabs,
        in_specs=[SMEM_SPEC, ANY_SPEC] + [VMEM_SPEC] * 2 + [ANY_SPEC] * 10,
        out_specs=[VMEM_SPEC] * (1 + slabs),
        scratch_shapes=[
            pltpu.VMEM((rank, order), jnp.float32),
            pltpu.VMEM((order, order), jnp.float32),
            pltpu.VMEM((rank, order), jnp.float32),
            pltpu.VMEM((rank, rank), jnp.float32),
            pltpu.VMEM((pairs, order, width), jnp.bfloat16),
            pltpu.VMEM((pairs, order, width), jnp.bfloat16),
            pltpu.VMEM((rank, width), jnp.float32),
            pltpu.SemaphoreType.DMA((12,)),
        ],
        compiler_params=params(24),
        name="subspace",
    )(place, diagonal, head, start, *cross, *fields)


def split(value):
    high = value.astype(jnp.bfloat16)
    return high, (value - high.astype(jnp.float32)).astype(jnp.bfloat16)


def dot3(left, right, contract):
    (a, b), (c, d) = left, right

    def dot(u, v):
        return lax.dot_general(u, v, (contract, ((), ())), preferred_element_type=jnp.float32)

    return dot(a, c) + (dot(a, d) + dot(b, c))


def pick(parts, rows):
    return parts[0][rows], parts[1][rows]


def project(place_ref, basis_ref, high_ref, low_ref, own_rows_ref, slab_refs, value_ref):
    z, index = place_ref[3], place_ref[4]
    high, low = split(basis_ref[...])
    slabs = len(slab_refs)
    rows, width = slab_refs[0].shape[2:]

    def dot(left, right):
        return lax.dot_general(left, right, (NN, ((), ())), preferred_element_type=jnp.float32)

    for number in range(high_ref.shape[0]):
        field_high, field_low = high_ref[number], low_ref[number]
        value_ref[...] = dot(high, field_high) + (dot(high, field_low) + dot(low, field_high))
        for step in range(slabs):
            at = pl.multiple_of(lax.rem(z + step, slabs) * rows, 8)
            for j in range(2):
                slab_refs[step][2 * number + j, 0] = value_ref[
                    pl.ds(at, rows), width * j : width * (j + 1)
                ]
    count_rows = own_rows_ref.shape[0]
    per_tile = 128 // count_rows
    tile = basis_ref[:, pl.ds(pl.multiple_of(index // per_tile * 128, 128), 128)].T
    shift = lax.rem(index, per_tile)
    value_ref[:, :width] = tile
    own_rows_ref[...] = value_ref[pl.ds(pl.multiple_of(shift * count_rows, 8), count_rows), :width]


def halves_kernel(count, place_ref, *refs):
    got_refs, kept_refs, (high_ref, low_ref) = refs[:count], refs[count : 2 * count], refs[2 * count :]
    x = place_ref[0]
    half = got_refs[0].shape[2]
    for number, pair in enumerate(species_pairs(got_refs)):
        for sources, owner in ((kept_refs, x), (got_refs, 1 - x)):
            value = jnp.concatenate([sources[i][s, 0] for i, s in pair], axis=1)
            rows = pl.ds(pl.multiple_of(owner * half, 128), half)
            high_ref[number, rows, :], low_ref[number, rows, :] = split(value)


def field_halves(place, got, kept):
    species = sum(piece.shape[0] for piece in got)
    half, width = got[0].shape[2:]
    shape = jax.ShapeDtypeStruct((species // 2, 2 * half, 2 * width), jnp.bfloat16)
    return pl.pallas_call(
        functools.partial(halves_kernel, len(got)),
        out_shape=[shape] * 2,
        in_specs=[SMEM_SPEC] + [VMEM_SPEC] * (2 * len(got)),
        out_specs=[VMEM_SPEC] * 2,
        compiler_params=params(24),
        name="field_halves",
    )(place, *got, *kept)


def own_kernel(place_ref, field_ref, keep_ref, send_ref, total_ref):
    half = field_ref.shape[2]
    side = half // 4
    values = split(jnp.concatenate([field_ref[s, 0] for s in range(field_ref.shape[0])], axis=1))

    @pl.when(pl.program_id(0) == 0)
    def _():
        total_ref[...] = jnp.zeros_like(total_ref)

    upper = dot3(pick(values, slice(0, 2 * side)), pick(values, slice(0, 2 * side)), NT)
    below = dot3(pick(values, slice(2 * side, half)), values, NT)
    total_ref[:side, :] += below[side:]
    total_ref[side : 2 * side, : 3 * side] += below[:side, : 3 * side]
    total_ref[side : 2 * side, 3 * side :] += upper[:side, :side]
    total_ref[2 * side :, : 2 * side] += upper[side : side + side // 2]
    total_ref[2 * side :, 2 * side :] += upper[side + side // 2 :]

    @pl.when(pl.program_id(0) == pl.num_programs(0) - 1)
    def _():
        rows = keep_ref.shape[0]
        core = place_ref[2]
        keep_ref[...] = total_ref[pl.ds(pl.multiple_of(core * rows, 8), rows), :]
        send_ref[...] = total_ref[pl.ds(pl.multiple_of((1 - core) * rows, 8), rows), :]


def own_blocks(place, field):
    half = field.shape[2]
    rows = 5 * half // 8
    step = math.gcd(field.shape[0], 4)
    shape = jax.ShapeDtypeStruct((rows // 2, half), jnp.float32)
    return pl.pallas_call(
        own_kernel,
        grid=(field.shape[0] // step,),
        out_shape=[shape, shape],
        in_specs=[SMEM_SPEC, pl.BlockSpec((step, 1, half, field.shape[3]), lambda i: (i, 0, 0, 0))],
        out_specs=[pl.BlockSpec((rows // 2, half), lambda i: (0, 0))] * 2,
        scratch_shapes=[pltpu.VMEM((rows, half), jnp.float32)],
        compiler_params=params(56),
        cost_estimate=pl.CostEstimate(flops=2 * 10**11, bytes_accessed=field.size * 4, transcendentals=0),
        name="own_blocks",
    )(place, field)


def species_pairs(refs):
    slots = [(i, s) for i, ref in enumerate(refs) for s in range(ref.shape[0])]
    return [slots[i : i + 2] for i in range(0, len(slots), 2)]


def cross_kernel(count, last, halves, place_ref, *refs):
    got_refs, kept_refs = refs[:count], refs[count : 2 * count]
    refs = refs[2 * count :]
    x, core = place_ref[0], place_ref[2]
    half = got_refs[0].shape[2]
    rows = half // 2
    in_order = x == 0

    def product(at):
        total = None
        some, every = pl.ds(at, rows), slice(None)
        for pair in species_pairs(got_refs):
            def two(refs, where):
                return jnp.concatenate([refs[i][s, 0, where, :] for i, s in pair], axis=1)

            low = split(jnp.where(in_order, two(kept_refs, some), two(got_refs, some)))
            high = split(jnp.where(in_order, two(got_refs, every), two(kept_refs, every)))
            value = dot3(low, high, NT)
            total = value if total is None else total + value
        return total

    for name, so_far, out in zip(halves, refs, refs[-len(halves) :]):
        at = pl.multiple_of((core if name == "keep" else 1 - core) * rows, 8)
        out[...] = product(at) + so_far[...] if last else product(at)


def cross_block(place, got, kept, halves, so_far=()):
    half = got[0].shape[2]
    shape = jax.ShapeDtypeStruct((half // 2, half), jnp.float32)
    return pl.pallas_call(
        functools.partial(cross_kernel, len(got), bool(so_far), halves),
        out_shape=[shape] * len(halves),
        in_specs=[SMEM_SPEC] + [VMEM_SPEC] * (2 * len(got) + len(so_far)),
        out_specs=[VMEM_SPEC] * len(halves),
        compiler_params=params(24),
        name="cross_block",
    )(place, *got, *kept, *so_far)


def quarters_kernel(place_ref, left_ref, right_ref, *out_refs):
    rows = out_refs[0].shape[0]
    x, y = place_ref[0], place_ref[1]
    for ref, (dx, dy) in zip(out_refs, ((0, 0),) + CORNERS):
        some = pl.ds(pl.multiple_of(((x ^ dx) * 2 + (y ^ dy)) * rows, 8), rows)
        ref[...] = left_ref[some, :] + right_ref[some, :]


def sum_quarters(place, left, right):
    shape = jax.ShapeDtypeStruct((left.shape[0] // 4, left.shape[1]), jnp.float32)
    return pl.pallas_call(
        quarters_kernel,
        out_shape=[shape] * 4,
        in_specs=[SMEM_SPEC] + [VMEM_SPEC] * 2,
        out_specs=[VMEM_SPEC] * 4,
        compiler_params=params(24),
        name="quarters",
    )(place, left, right)


def join_kernel(place_ref, *refs):
    *slab_refs, out_ref, sems = refs
    slabs = len(slab_refs)
    width = slab_refs[0].shape[3]
    copies = []
    for step in range(slabs):
        source = lax.rem(place_ref[3] + slabs - step, slabs)
        target = out_ref.at[:, :, :, pl.ds(pl.multiple_of(source * width, 128), width)]
        copies.append(pltpu.make_async_copy(slab_refs[step], target, sems.at[step]))
    for copy in copies:
        copy.start()
    for copy in copies:
        copy.wait()


def join_slabs(place, slabs):
    shape = slabs[0].shape[:3] + (slabs[0].shape[3] * len(slabs),)
    return pl.pallas_call(
        join_kernel,
        out_shape=jax.ShapeDtypeStruct(shape, jnp.float32),
        in_specs=[SMEM_SPEC] + [VMEM_SPEC] * len(slabs),
        out_specs=ANY_SPEC,
        scratch_shapes=[pltpu.SemaphoreType.DMA((len(slabs),))],
        compiler_params=params(24),
        name="join",
    )(place, *slabs)


def blocks(array, count):
    return array.reshape((count, array.shape[0] // count) + array.shape[1:])


def part(array, index):
    return lax.dynamic_index_in_dim(array, index, 0, keepdims=False)


def flip(size, bit):
    return [(i, i ^ bit) for i in range(size)]


def turn(size, step):
    return [(i, (i + step) % size) for i in range(size)]


def after(value, *others):
    return lax.optimization_barrier((value, others))[0]


def send_core(array):
    return lax.ppermute(array, "sa", flip(lax.axis_size("sa"), 1))


def send_corner(array, dx, dy):
    size = lax.axis_size("sa")
    pairs = [(x * size + s, (x ^ dx) * size + (s ^ (2 * dy))) for x in range(2) for s in range(size)]
    return lax.ppermute(array, ("gx", "sa"), pairs)


def sum_z(array, *others):
    size = lax.axis_size("gy")
    shares = [lax.ppermute(array, "gy", turn(size, step)) for step in range(size - 1, 0, -1)]
    return sum(after(shares, others), array)


def chunk_sizes(species):
    return [3, species - 5, 2]


def on_halves(field, start):
    x = lax.axis_index("gx")
    y = lax.axis_index("sa") // 2
    core = lax.axis_index("sa") % 2
    z = lax.axis_index("gy")
    place = jnp.stack([x, y, core, z, lax.axis_index(("gx", "gy", "sa"))]).astype(jnp.int32)
    species = field.shape[0] // 2
    columns = field.shape[0] * field.shape[1] * field.shape[3]
    columns = columns * lax.axis_size("gy") * lax.axis_size("sa")
    sizes = chunk_sizes(species)
    starts = [sum(sizes[:i]) for i in range(len(sizes))]

    def chunk(source, owner, i):
        return lax.dynamic_slice_in_dim(source, owner * species + starts[i], sizes[i], 0)

    sent = [chunk(field, 1 - x, 0)]
    rest = after(field, sent[0])
    sent = sent + [chunk(rest, 1 - x, i) for i in range(1, len(sizes))]
    got = [lax.ppermute(piece, "gx", flip(2, 1)) for piece in sent]

    own_field = after(rest, sent)
    own_keep, own_send = own_blocks(place, own_field)
    own = blocks(after(own_keep + send_core(own_send), got[0]), 2)
    own = part(own, y) + send_corner(part(own, 1 - y), 0, 1)
    kept = [chunk(own_field, x, i) for i in range(len(sizes))]
    start_t = start.T
    *early_got, final_got = got
    so_far_send, so_far_keep = cross_block(place, early_got, kept[:-1], ("send", "keep"))
    own = sum_z(own, so_far_send, so_far_keep, kept, start_t)
    beside = send_corner(own, 0, 1)

    final_got = after(final_got, own)
    (cross_send,) = cross_block(place, [final_got], kept[-1:], ("send",), (so_far_send,))
    cross_sent = send_core(after(cross_send, beside))
    (cross_keep,) = cross_block(
        place, [final_got], kept[-1:], ("keep",), (after(so_far_keep, cross_send),)
    )
    cross, *shares = sum_quarters(place, cross_keep, cross_sent)
    shares = [send_corner(share, dx, dy) for share, (dx, dy) in zip(shares, CORNERS)]
    own, beside = after((own, beside), shares[0])
    cross = sum(shares, cross)
    own_pieces = [own, send_corner(own, 1, 0), beside, send_corner(beside, 1, 0)]
    own_pieces = own_pieces + [send_core(piece) for piece in own_pieces]
    fields = field_halves(place, early_got + [final_got], kept)
    cross = sum_z(cross, own_pieces[:4], fields)
    diagonal, head = diagonal_blocks(place, own_pieces, start_t)
    across = {(dx, dy): send_corner(cross, dx, dy) for dx, dy in CORNERS[::-1]}
    near = [after(across[corner], head) for corner in CORNERS]
    cross_pieces = [cross] + near + [send_core(piece) for piece in [cross] + near]

    slabs = lax.axis_size("gy")
    own_rows, *projected = subspace_pieces(
        place,
        diagonal,
        head,
        start_t,
        cross_pieces,
        fields,
        1.0 / columns,
        slabs,
        start.shape[0] // lax.axis_size(("gx", "gy", "sa")),
    )
    arrived = [projected[0]] + [
        lax.ppermute(projected[i], "gy", turn(slabs, i)) for i in range(1, slabs)
    ]
    return join_slabs(place, arrived), own_rows


def outer(left, right):
    return jnp.einsum(
        "stxy,stzy->xz", left, right, precision=HIGH_PREC, preferred_element_type=jnp.float32
    )


def on_fibres(field, start):
    axes = ("gx", "gy", "sa")
    fibres = lax.all_to_all(field, "gx", split_axis=0, concat_axis=2, tiled=True)
    columns = fibres.shape[0] * fibres.shape[1] * fibres.shape[3] * lax.axis_size(axes)
    gram = lax.psum(outer(fibres, fibres), axes) / columns
    basis = subspace_whole(gram, start.T)
    projected = jnp.einsum(
        "kx,stxy->stky", basis, fibres, precision=HIGH_PREC, preferred_element_type=jnp.float32
    )
    rows_dev = start.shape[0] // lax.axis_size(axes)
    own_rows = lax.dynamic_slice_in_dim(basis.T, lax.axis_index(axes) * rows_dev, rows_dev, 0)
    return lax.all_to_all(projected, "gy", split_axis=2, concat_axis=3, tiled=True), own_rows


def on_device(scalar_field, start_basis):
    if lax.axis_size("gx") == 2 and lax.axis_size("sa") == 4:
        return on_halves(scalar_field, start_basis)
    return on_fibres(scalar_field, start_basis)


def solution(mesh):
    placed = (P("sa", None, "gx", "gy"), P())
    return jax.shard_map(
        on_device,
        mesh=mesh,
        in_specs=placed,
        out_specs=(P(("sa", "gx"), None, "gy", None), P(("gx", "gy", "sa"), None)),
        check_vma=False,
    )
```

```python
import functools
import math

import jax
import jax.numpy as jnp
from jax import lax
from jax.experimental import pallas as pl
from jax.experimental.pallas import tpu as pltpu
from jax.sharding import PartitionSpec as P

ITERS = 3
CORNERS = ((1, 0), (0, 1), (1, 1))
PANEL = 8
AHEAD = 3
SMALL = 1e-4
MEDIUM = 4e-4
NN = ((1,), (0,))
NT = ((1,), (1,))
HIGHEST_PREC = lax.Precision.HIGHEST
HIGH_PREC = lax.Precision.HIGH


def mul(left, right):
    return lax.dot_general(
        left, right, (((1,), (0,)), ((), ())), precision=HIGHEST_PREC, preferred_element_type=jnp.float32
    )


def mul_t(left, right):
    return lax.dot_general(
        left, right, (((1,), (1,)), ((), ())), precision=HIGHEST_PREC, preferred_element_type=jnp.float32
    )


def three_parts(value):
    high = value.astype(jnp.bfloat16)
    rest = value - high.astype(jnp.float32)
    middle = rest.astype(jnp.bfloat16)
    return high, middle, (rest - middle.astype(jnp.float32)).astype(jnp.bfloat16)


def inverse_factor(matrix):
    order = matrix.shape[0]
    panels = order // PANEL
    shape = (PANEL, order)
    sub = lax.broadcasted_iota(jnp.int32, shape, 0)
    lane = lax.broadcasted_iota(jnp.int32, shape, 1)
    rows = [matrix[PANEL * q : PANEL * (q + 1), :] for q in range(panels)]

    def spread(q, p):
        return [
            jnp.broadcast_to(rows[q][:, PANEL * p + j : PANEL * p + j + 1], shape) for j in range(PANEL)
        ]

    def sublane(value, k):
        return jnp.broadcast_to(value[k : k + 1, :], shape)

    following = spread(0, 0)
    for p in range(panels):
        near = list(range(p + 1, min(p + 1 + AHEAD, panels)))
        columns = {q: spread(q, p) for q in near}
        columns[p] = following
        following = spread(p + 1, p + 1) if near else []
        inside = (lane >= PANEL * p) & (lane < PANEL * (p + 1))
        rows[p] = jnp.where(inside, jnp.where(lane == sub + PANEL * p, 1.0, 0.0), rows[p])
        for q in range(p + 1, panels):
            rows[q] = jnp.where(inside, 0.0, rows[q])
        for j in range(PANEL):
            scale = lax.rsqrt(sublane(columns[p][j], j))
            factor = {q: columns[q][j] * scale for q in [p] + near}
            row = sublane(rows[p], j) * scale
            for k in range(j + 1, PANEL):
                pivot = sublane(factor[p], k)
                for q in [p] + near:
                    columns[q][k] = columns[q][k] - factor[q] * pivot
            for k in range(len(following)):
                following[k] = following[k] - factor[p + 1] * sublane(factor[p + 1], k)
            below = jnp.where(sub > j, factor[p], 0.0)
            rows[p] = jnp.where(sub == j, row, rows[p] - below * row)
            for q in near:
                rows[q] = rows[q] - factor[q] * row
        if p + 1 + AHEAD < panels:
            high, middle, low = (part.astype(jnp.float32) for part in three_parts(rows[p]))
            left = jnp.concatenate([high, high, high, middle, middle, low], axis=0)
            right = jnp.concatenate([high, middle, low, high, middle, high], axis=0)
            update = lax.dot_general(
                left.astype(jnp.bfloat16),
                right.astype(jnp.bfloat16),
                (((0,), (0,)), ((), ())),
                preferred_element_type=jnp.float32,
            )
            for q in range(p + 1 + AHEAD, panels):
                rows[q] = rows[q] - update[PANEL * q : PANEL * (q + 1), :]
    return jnp.concatenate(
        [jnp.where(lane <= sub + PANEL * q, rows[q], 0.0) for q in range(panels)], axis=0
    )


def lower(matrix, row, col):
    return jnp.where(row > col, matrix, jnp.where(row == col, 0.5 * matrix, 0.0))


def inverse_factor_near_one(error, row, col):
    first = lower(error, row, col)
    eye = jnp.where(row == col, 1.0, 0.0)
    part = first.astype(jnp.bfloat16)
    square = lax.dot_general(part, part, (NN, ((), ())), preferred_element_type=jnp.float32)
    return eye - first + (lower(dot_t(part, part), row, col) + square)


def dot_t(left, right):
    return lax.dot_general(left, right, (NT, ((), ())), preferred_element_type=jnp.float32)


def inner_products(value):
    high, middle, low = three_parts(value)
    mixed = dot_t(high, middle) + dot_t(high, low)
    return dot_t(high, high) + ((mixed + mixed.T) + dot_t(middle, middle))


def apply(factor, value):
    a, b, c = three_parts(factor)
    high, middle, low = three_parts(value)

    def pass_of(left, right):
        return lax.dot_general(
            jnp.concatenate(left, axis=1),
            jnp.concatenate(right, axis=0),
            (NN, ((), ())),
            preferred_element_type=jnp.float32,
        )

    return pass_of([a, b], [high, middle]) + (
        pass_of([a, b], [middle, high]) + pass_of([a, c], [low, high])
    )


def iterate(scale, first_map, start_ref, basis_ref, gram_ref, inverse_ref, mapped_ref):
    rank = start_ref.shape[0]
    row = lax.broadcasted_iota(jnp.int32, (rank, rank), 0)
    col = lax.broadcasted_iota(jnp.int32, (rank, rank), 1)
    eye = jnp.where(row == col, 1.0, 0.0)
    first_map()

    def iteration(last):
        mapped = mapped_ref[...] * scale
        once = apply(inverse_factor(inner_products(mapped)), mapped)
        source = once if last else mul(once, gram_ref[...])
        inner = inner_products(once)
        error = inner - eye
        size = jnp.sum(error * error)
        inverse_ref[...] = inverse_factor_near_one(error, row, col)

        @pl.when(jnp.logical_and(size > SMALL, size <= MEDIUM))
        def _():
            about = inverse_ref[...]
            rest = mul_t(mul(about, inner), about) - eye
            inverse_ref[...] = about - mul(lower(rest, row, col), about)

        @pl.when(jnp.logical_not(size <= MEDIUM))
        def _():
            inverse_ref[...] = inverse_factor(inner)

        target_ref = basis_ref if last else mapped_ref
        target_ref[...] = apply(inverse_ref[...], source)

    def step(_, carry):
        iteration(False)
        return carry

    lax.fori_loop(0, ITERS - 1, step, 0)
    iteration(True)


VMEM_SPEC = pl.BlockSpec(memory_space=pltpu.VMEM)
SMEM_SPEC = pl.BlockSpec(memory_space=pltpu.SMEM)
ANY_SPEC = pl.BlockSpec(memory_space=pl.ANY)


def params(mebibytes):
    return pltpu.CompilerParams(vmem_limit_bytes=mebibytes << 20)


def whole_kernel(gram_ref, start_ref, basis_ref, inverse_ref, mapped_ref):
    def first_map():
        mapped_ref[...] = mul(start_ref[...], gram_ref[...])

    iterate(1.0, first_map, start_ref, basis_ref, gram_ref, inverse_ref, mapped_ref)


def subspace_whole(gram, start):
    rank, order = start.shape
    return pl.pallas_call(
        whole_kernel,
        out_shape=jax.ShapeDtypeStruct((rank, order), jnp.float32),
        in_specs=[VMEM_SPEC] * 2,
        out_specs=VMEM_SPEC,
        scratch_shapes=[pltpu.VMEM((rank, rank), jnp.float32), pltpu.VMEM((rank, order), jnp.float32)],
        compiler_params=params(24),
        name="subspace_whole",
    )(gram, start)


def diagonal_kernel(place_ref, *refs):
    own_refs, (start_ref, gram_ref, head_ref, packed_ref) = refs[:8], refs[8:]
    x, y, core = place_ref[0], place_ref[1], place_ref[2]
    half = gram_ref.shape[1]
    side = half // 4
    for ref, (dc, dx, dy) in zip(own_refs, PIECES):
        rows = ref.shape[0]
        at = pl.multiple_of(((core ^ dc) * 2 + (y ^ dy)) * rows, 8)
        packed_ref[x ^ dx, pl.ds(at, rows), :] = ref[...]
    at = [side * i for i in range(5)]
    for p in range(2):
        last = packed_ref[p, :side, :]
        third = packed_ref[p, side : 2 * side, :]
        gram_ref[p, at[3] : at[4], at[0] : at[4]] = last
        gram_ref[p, at[0] : at[3], at[3] : at[4]] = last[:, : 3 * side].T
        gram_ref[p, at[2] : at[3], at[0] : at[3]] = third[:, : 3 * side]
        gram_ref[p, at[0] : at[2], at[2] : at[3]] = third[:, : 2 * side].T
        gram_ref[p, at[0] : at[1], at[0] : at[1]] = third[:, 3 * side :]
        second = packed_ref[p, 2 * side :, :]
        second = jnp.concatenate([second[:, : 2 * side], second[:, 2 * side :]], axis=0)
        gram_ref[p, at[1] : at[2], at[0] : at[2]] = second
        gram_ref[p, at[0] : at[1], at[1] : at[2]] = second[:, :side].T
        columns = slice(half * p, half * (p + 1))
        head_ref[:, columns] = mul(start_ref[:, columns], gram_ref[p])


def diagonal_blocks(place, own, start):
    rank, order = start.shape
    half = order // 2
    return pl.pallas_call(
        diagonal_kernel,
        out_shape=[
            jax.ShapeDtypeStruct((2, half, half), jnp.float32),
            jax.ShapeDtypeStruct((rank, order), jnp.float32),
        ],
        in_specs=[SMEM_SPEC] + [VMEM_SPEC] * 9,
        out_specs=[VMEM_SPEC] * 2,
        scratch_shapes=[pltpu.VMEM((2, 5 * half // 8, half), jnp.float32)],
        compiler_params=params(16),
        name="diagonal",
    )(place, *own, start)


def pieces_kernel(scale, place_ref, *refs):
    diagonal_ref, head_ref, start_ref, refs = refs[0], refs[1], refs[2], refs[3:]
    cross_refs, refs = refs[:8], refs[8:]
    field_refs, refs = refs[:2], refs[2:]
    own_rows_ref, *slab_refs = refs[:-8]
    basis_ref, gram_ref, mapped_ref, inverse_ref, high_ref, low_ref, value_ref, sems = refs[-8:]
    x, y, core = place_ref[0], place_ref[1], place_ref[2]
    half = gram_ref.shape[0] // 2
    cross_copies, later_copies = [], []
    for index, (dc, dx, dy) in enumerate(PIECES):
        rows = cross_refs[index].shape[0]
        at = pl.multiple_of(((core ^ dc) * 4 + (x ^ dx) * 2 + (y ^ dy)) * rows, 8)
        cross_copies.append(
            pltpu.make_async_copy(
                cross_refs[index], gram_ref.at[pl.ds(at, rows), half:], sems.at[index]
            )
        )
    for p in range(2):
        square = pl.ds(half * p, half)
        later_copies.append(
            pltpu.make_async_copy(diagonal_ref.at[p], gram_ref.at[square, square], sems.at[8 + p])
        )
    for index, (source, target) in enumerate(zip(field_refs, (high_ref, low_ref))):
        later_copies.append(pltpu.make_async_copy(source, target, sems.at[10 + index]))
    for copy in cross_copies + later_copies:
        copy.start()
    for copy in cross_copies:
        copy.wait()
    gram_ref[half:, :half] = gram_ref[:half, half:].T

    def first_map():
        mapped_ref[:, :half] = head_ref[:, :half] + mul(start_ref[:, half:], gram_ref[half:, :half])
        mapped_ref[:, half:] = head_ref[:, half:] + mul(start_ref[:, :half], gram_ref[:half, half:])
        for copy in later_copies:
            copy.wait()

    iterate(scale, first_map, start_ref, basis_ref, gram_ref, inverse_ref, mapped_ref)
    project(place_ref, basis_ref, high_ref, low_ref, own_rows_ref, slab_refs, value_ref)


PIECES = [(dc, dx, dy) for dc in range(2) for dx, dy in ((0, 0), (1, 0), (0, 1), (1, 1))]


def subspace_pieces(place, diagonal, head, start, cross, fields, scale, slabs, own_rows):
    rank, order = start.shape
    pairs, _, width = fields[0].shape
    slab = jax.ShapeDtypeStruct((2 * pairs, 1, rank // slabs, width // 2), jnp.float32)
    return pl.pallas_call(
        functools.partial(pieces_kernel, scale),
        out_shape=[jax.ShapeDtypeStruct((own_rows, rank), jnp.float32)] + [slab] * slabs,
        in_specs=[SMEM_SPEC, ANY_SPEC] + [VMEM_SPEC] * 2 + [ANY_SPEC] * 10,
        out_specs=[VMEM_SPEC] * (1 + slabs),
        scratch_shapes=[
            pltpu.VMEM((rank, order), jnp.float32),
            pltpu.VMEM((order, order), jnp.float32),
            pltpu.VMEM((rank, order), jnp.float32),
            pltpu.VMEM((rank, rank), jnp.float32),
            pltpu.VMEM((pairs, order, width), jnp.bfloat16),
            pltpu.VMEM((pairs, order, width), jnp.bfloat16),
            pltpu.VMEM((rank, width), jnp.float32),
            pltpu.SemaphoreType.DMA((12,)),
        ],
        compiler_params=params(24),
        name="subspace",
    )(place, diagonal, head, start, *cross, *fields)


def split(value):
    high = value.astype(jnp.bfloat16)
    return high, (value - high.astype(jnp.float32)).astype(jnp.bfloat16)


def dot3(left, right, contract):
    (a, b), (c, d) = left, right

    def dot(u, v):
        return lax.dot_general(u, v, (contract, ((), ())), preferred_element_type=jnp.float32)

    return dot(a, c) + (dot(a, d) + dot(b, c))


def pick(parts, rows):
    return parts[0][rows], parts[1][rows]


def project(place_ref, basis_ref, high_ref, low_ref, own_rows_ref, slab_refs, value_ref):
    z, index = place_ref[3], place_ref[4]
    high, low = split(basis_ref[...])
    slabs = len(slab_refs)
    rows, width = slab_refs[0].shape[2:]

    def dot(left, right):
        return lax.dot_general(left, right, (NN, ((), ())), preferred_element_type=jnp.float32)

    for number in range(high_ref.shape[0]):
        field_high, field_low = high_ref[number], low_ref[number]
        value_ref[...] = dot(high, field_high) + (dot(high, field_low) + dot(low, field_high))
        for step in range(slabs):
            at = pl.multiple_of(lax.rem(z + step, slabs) * rows, 8)
            for j in range(2):
                slab_refs[step][2 * number + j, 0] = value_ref[
                    pl.ds(at, rows), width * j : width * (j + 1)
                ]
    count_rows = own_rows_ref.shape[0]
    per_tile = 128 // count_rows
    tile = basis_ref[:, pl.ds(pl.multiple_of(index // per_tile * 128, 128), 128)].T
    shift = lax.rem(index, per_tile)
    value_ref[:, :width] = tile
    own_rows_ref[...] = value_ref[pl.ds(pl.multiple_of(shift * count_rows, 8), count_rows), :width]


def halves_kernel(count, place_ref, *refs):
    got_refs, kept_refs, (high_ref, low_ref) = refs[:count], refs[count : 2 * count], refs[2 * count :]
    x = place_ref[0]
    half = got_refs[0].shape[2]
    for number, pair in enumerate(species_pairs(got_refs)):
        for sources, owner in ((kept_refs, x), (got_refs, 1 - x)):
            value = jnp.concatenate([sources[i][s, 0] for i, s in pair], axis=1)
            rows = pl.ds(pl.multiple_of(owner * half, 128), half)
            high_ref[number, rows, :], low_ref[number, rows, :] = split(value)


def field_halves(place, got, kept):
    species = sum(piece.shape[0] for piece in got)
    half, width = got[0].shape[2:]
    shape = jax.ShapeDtypeStruct((species // 2, 2 * half, 2 * width), jnp.bfloat16)
    return pl.pallas_call(
        functools.partial(halves_kernel, len(got)),
        out_shape=[shape] * 2,
        in_specs=[SMEM_SPEC] + [VMEM_SPEC] * (2 * len(got)),
        out_specs=[VMEM_SPEC] * 2,
        compiler_params=params(24),
        name="field_halves",
    )(place, *got, *kept)


def own_kernel(place_ref, field_ref, keep_ref, send_ref, total_ref):
    half = field_ref.shape[2]
    side = half // 4
    values = split(jnp.concatenate([field_ref[s, 0] for s in range(field_ref.shape[0])], axis=1))

    @pl.when(pl.program_id(0) == 0)
    def _():
        total_ref[...] = jnp.zeros_like(total_ref)

    upper = dot3(pick(values, slice(0, 2 * side)), pick(values, slice(0, 2 * side)), NT)
    below = dot3(pick(values, slice(2 * side, half)), values, NT)
    total_ref[:side, :] += below[side:]
    total_ref[side : 2 * side, : 3 * side] += below[:side, : 3 * side]
    total_ref[side : 2 * side, 3 * side :] += upper[:side, :side]
    total_ref[2 * side :, : 2 * side] += upper[side : side + side // 2]
    total_ref[2 * side :, 2 * side :] += upper[side + side // 2 :]

    @pl.when(pl.program_id(0) == pl.num_programs(0) - 1)
    def _():
        rows = keep_ref.shape[0]
        core = place_ref[2]
        keep_ref[...] = total_ref[pl.ds(pl.multiple_of(core * rows, 8), rows), :]
        send_ref[...] = total_ref[pl.ds(pl.multiple_of((1 - core) * rows, 8), rows), :]


def own_blocks(place, field):
    half = field.shape[2]
    rows = 5 * half // 8
    step = math.gcd(field.shape[0], 4)
    shape = jax.ShapeDtypeStruct((rows // 2, half), jnp.float32)
    return pl.pallas_call(
        own_kernel,
        grid=(field.shape[0] // step,),
        out_shape=[shape, shape],
        in_specs=[SMEM_SPEC, pl.BlockSpec((step, 1, half, field.shape[3]), lambda i: (i, 0, 0, 0))],
        out_specs=[pl.BlockSpec((rows // 2, half), lambda i: (0, 0))] * 2,
        scratch_shapes=[pltpu.VMEM((rows, half), jnp.float32)],
        compiler_params=params(56),
        cost_estimate=pl.CostEstimate(flops=2 * 10**11, bytes_accessed=field.size * 4, transcendentals=0),
        name="own_blocks",
    )(place, field)


def species_pairs(refs):
    slots = [(i, s) for i, ref in enumerate(refs) for s in range(ref.shape[0])]
    return [slots[i : i + 2] for i in range(0, len(slots), 2)]


def cross_kernel(count, last, halves, place_ref, *refs):
    got_refs, kept_refs = refs[:count], refs[count : 2 * count]
    refs = refs[2 * count :]
    x, core = place_ref[0], place_ref[2]
    half = got_refs[0].shape[2]
    rows = half // 2
    in_order = x == 0

    def product(at):
        total = None
        some, every = pl.ds(at, rows), slice(None)
        for pair in species_pairs(got_refs):
            def two(refs, where):
                return jnp.concatenate([refs[i][s, 0, where, :] for i, s in pair], axis=1)

            low = split(jnp.where(in_order, two(kept_refs, some), two(got_refs, some)))
            high = split(jnp.where(in_order, two(got_refs, every), two(kept_refs, every)))
            value = dot3(low, high, NT)
            total = value if total is None else total + value
        return total

    for name, so_far, out in zip(halves, refs, refs[-len(halves) :]):
        at = pl.multiple_of((core if name == "keep" else 1 - core) * rows, 8)
        out[...] = product(at) + so_far[...] if last else product(at)


def cross_block(place, got, kept, halves, so_far=()):
    half = got[0].shape[2]
    shape = jax.ShapeDtypeStruct((half // 2, half), jnp.float32)
    return pl.pallas_call(
        functools.partial(cross_kernel, len(got), bool(so_far), halves),
        out_shape=[shape] * len(halves),
        in_specs=[SMEM_SPEC] + [VMEM_SPEC] * (2 * len(got) + len(so_far)),
        out_specs=[VMEM_SPEC] * len(halves),
        compiler_params=params(24),
        name="cross_block",
    )(place, *got, *kept, *so_far)


def quarters_kernel(place_ref, left_ref, right_ref, *out_refs):
    rows = out_refs[0].shape[0]
    x, y = place_ref[0], place_ref[1]
    for ref, (dx, dy) in zip(out_refs, ((0, 0),) + CORNERS):
        some = pl.ds(pl.multiple_of(((x ^ dx) * 2 + (y ^ dy)) * rows, 8), rows)
        ref[...] = left_ref[some, :] + right_ref[some, :]


def sum_quarters(place, left, right):
    shape = jax.ShapeDtypeStruct((left.shape[0] // 4, left.shape[1]), jnp.float32)
    return pl.pallas_call(
        quarters_kernel,
        out_shape=[shape] * 4,
        in_specs=[SMEM_SPEC] + [VMEM_SPEC] * 2,
        out_specs=[VMEM_SPEC] * 4,
        compiler_params=params(24),
        name="quarters",
    )(place, left, right)


def join_kernel(place_ref, *refs):
    *slab_refs, out_ref, sems = refs
    slabs = len(slab_refs)
    width = slab_refs[0].shape[3]
    copies = []
    for step in range(slabs):
        source = lax.rem(place_ref[3] + slabs - step, slabs)
        target = out_ref.at[:, :, :, pl.ds(pl.multiple_of(source * width, 128), width)]
        copies.append(pltpu.make_async_copy(slab_refs[step], target, sems.at[step]))
    for copy in copies:
        copy.start()
    for copy in copies:
        copy.wait()


def join_slabs(place, slabs):
    shape = slabs[0].shape[:3] + (slabs[0].shape[3] * len(slabs),)
    return pl.pallas_call(
        join_kernel,
        out_shape=jax.ShapeDtypeStruct(shape, jnp.float32),
        in_specs=[SMEM_SPEC] + [VMEM_SPEC] * len(slabs),
        out_specs=ANY_SPEC,
        scratch_shapes=[pltpu.SemaphoreType.DMA((len(slabs),))],
        compiler_params=params(24),
        name="join",
    )(place, *slabs)


def blocks(array, count):
    return array.reshape((count, array.shape[0] // count) + array.shape[1:])


def part(array, index):
    return lax.dynamic_index_in_dim(array, index, 0, keepdims=False)


def flip(size, bit):
    return [(i, i ^ bit) for i in range(size)]


def turn(size, step):
    return [(i, (i + step) % size) for i in range(size)]


def after(value, *others):
    return lax.optimization_barrier((value, others))[0]


def send_core(array):
    return lax.ppermute(array, "sa", flip(lax.axis_size("sa"), 1))


def send_corner(array, dx, dy):
    size = lax.axis_size("sa")
    pairs = [(x * size + s, (x ^ dx) * size + (s ^ (2 * dy))) for x in range(2) for s in range(size)]
    return lax.ppermute(array, ("gx", "sa"), pairs)


def sum_z(array, *others):
    size = lax.axis_size("gy")
    shares = [lax.ppermute(array, "gy", turn(size, step)) for step in range(size - 1, 0, -1)]
    return sum(after(shares, others), array)


def chunk_sizes(species):
    return [3, species - 5, 2]


def on_halves(field, start):
    x = lax.axis_index("gx")
    y = lax.axis_index("sa") // 2
    core = lax.axis_index("sa") % 2
    z = lax.axis_index("gy")
    place = jnp.stack([x, y, core, z, lax.axis_index(("gx", "gy", "sa"))]).astype(jnp.int32)
    species = field.shape[0] // 2
    columns = field.shape[0] * field.shape[1] * field.shape[3]
    columns = columns * lax.axis_size("gy") * lax.axis_size("sa")
    sizes = chunk_sizes(species)
    starts = [sum(sizes[:i]) for i in range(len(sizes))]

    def chunk(source, owner, i):
        return lax.dynamic_slice_in_dim(source, owner * species + starts[i], sizes[i], 0)

    sent = [chunk(field, 1 - x, 0)]
    rest = after(field, sent[0])
    sent = sent + [chunk(rest, 1 - x, i) for i in range(1, len(sizes))]
    got = [lax.ppermute(piece, "gx", flip(2, 1)) for piece in sent]

    own_field = after(rest, sent)
    own_keep, own_send = own_blocks(place, own_field)
    own = blocks(after(own_keep + send_core(own_send), got[0]), 2)
    own = part(own, y) + send_corner(part(own, 1 - y), 0, 1)
    kept = [chunk(own_field, x, i) for i in range(len(sizes))]
    start_t = start.T
    *early_got, final_got = got
    so_far_send, so_far_keep = cross_block(place, early_got, kept[:-1], ("send", "keep"))
    own = sum_z(own, so_far_send, so_far_keep, kept, start_t)
    beside = send_corner(own, 0, 1)

    final_got = after(final_got, own)
    (cross_send,) = cross_block(place, [final_got], kept[-1:], ("send",), (so_far_send,))
    cross_sent = send_core(after(cross_send, beside))
    (cross_keep,) = cross_block(
        place, [final_got], kept[-1:], ("keep",), (after(so_far_keep, cross_send),)
    )
    cross, *shares = sum_quarters(place, cross_keep, cross_sent)
    shares = [send_corner(share, dx, dy) for share, (dx, dy) in zip(shares, CORNERS)]
    own, beside = after((own, beside), shares[0])
    cross = sum(shares, cross)
    own_pieces = [own, send_corner(own, 1, 0), beside, send_corner(beside, 1, 0)]
    own_pieces = own_pieces + [send_core(piece) for piece in own_pieces]
    fields = field_halves(place, early_got + [final_got], kept)
    cross = sum_z(cross, own_pieces[:4], fields)
    diagonal, head = diagonal_blocks(place, own_pieces, start_t)
    across = {(dx, dy): send_corner(cross, dx, dy) for dx, dy in CORNERS[::-1]}
    near = [after(across[corner], head) for corner in CORNERS]
    cross_pieces = [cross] + near + [send_core(piece) for piece in [cross] + near]

    slabs = lax.axis_size("gy")
    own_rows, *projected = subspace_pieces(
        place,
        diagonal,
        head,
        start_t,
        cross_pieces,
        fields,
        1.0 / columns,
        slabs,
        start.shape[0] // lax.axis_size(("gx", "gy", "sa")),
    )
    arrived = [projected[0]] + [
        lax.ppermute(projected[i], "gy", turn(slabs, i)) for i in range(1, slabs)
    ]
    return join_slabs(place, arrived), own_rows


def outer(left, right):
    return jnp.einsum(
        "stxy,stzy->xz", left, right, precision=HIGH_PREC, preferred_element_type=jnp.float32
    )


def on_fibres(field, start):
    axes = ("gx", "gy", "sa")
    fibres = lax.all_to_all(field, "gx", split_axis=0, concat_axis=2, tiled=True)
    columns = fibres.shape[0] * fibres.shape[1] * fibres.shape[3] * lax.axis_size(axes)
    gram = lax.psum(outer(fibres, fibres), axes) / columns
    basis = subspace_whole(gram, start.T)
    projected = jnp.einsum(
        "kx,stxy->stky", basis, fibres, precision=HIGH_PREC, preferred_element_type=jnp.float32
    )
    rows_dev = start.shape[0] // lax.axis_size(axes)
    own_rows = lax.dynamic_slice_in_dim(basis.T, lax.axis_index(axes) * rows_dev, rows_dev, 0)
    return lax.all_to_all(projected, "gy", split_axis=2, concat_axis=3, tiled=True), own_rows


def on_device(scalar_field, start_basis):
    if lax.axis_size("gx") == 2 and lax.axis_size("sa") == 4:
        return on_halves(scalar_field, start_basis)
    return on_fibres(scalar_field, start_basis)


def solution(mesh):
    placed = (P("sa", None, "gx", "gy"), P())
    return jax.shard_map(
        on_device,
        mesh=mesh,
        in_specs=placed,
        out_specs=(P(("sa", "gx"), None, "gy", None), P(("gx", "gy", "sa"), None)),
        check_vma=False,
    )
```
